128 devices in a mesh: dp: 16 (over y_lo, z, core), tensor: 8 (over x, y_hi).
Axes of the slice: x: 4, y: 4 (y_hi: 2, y_lo: 2; y = y_hi * 2 + y_lo), z: 4, core: 2. Of those that a mesh axis runs over, the one named last changes fastest.
Arguments:
- teacher_queries: bfloat16 [16, 1024, 8192], P('dp', None, 'tensor'), may hold values from -100 to 100
- teacher_keys: bfloat16 [16, 1024, 1024], P('dp', None, 'tensor'), may hold values from -5 to 5
- teacher_values: bfloat16 [16, 1024, 1024], P('dp', None, 'tensor'), may hold values from -6 to 6
- projector: bfloat16 [8192, 4096], P('tensor'), may hold values from -0.25 to 0.25
- student_inputs: bfloat16 [16, 1024, 4096], P('dp', 'tensor'), may hold values from -30 to 30
- query_weight: bfloat16 [4096, 4096], P('dp', 'tensor'), may hold values from -1 to 1
- key_weight: bfloat16 [4096, 1024], P('dp', 'tensor'), may hold values from -1 to 1
- value_weight: bfloat16 [4096, 1024], P('dp', 'tensor'), may hold values from -0.09375 to 0.09375
Outputs:
- query_grad: float32 [4096, 4096], P('dp', 'tensor')
- key_grad: float32 [4096, 1024], P('dp', 'tensor')
- value_grad: float32 [4096, 1024], P('dp', 'tensor')
The draws below stay inside these ranges and needn't reach their ends.
All inputs are finite; a program needn't handle non-finite values.
Results may differ from the reference program's by a relative error of at most 0.029.
Values may be sent and summed in bfloat16 or wider, within the bound.
No kernel may reach another device: no remote copies, remote signals or barrier semaphores. Data moves between devices by JAX's collectives and lax.ppermute only.
A program may use at most 128 MiB of HBM per device.

```python
import jax
import jax.numpy as jnp
from jax import lax

TDIM = 8192
SDIM = 4096
HEAD = 128
TQH = 64
TKVH = 8
SQH = 32
SKVH = 8
SEQ = 1024
N_DP = 16
N_TENSOR = 8


def shared_keys(key):
    keys = jax.random.truncated_normal(key, -5.0, 5.0, (N_DP, SEQ, TKVH * HEAD), jnp.float32)
    position = jnp.arange(SEQ)[None, :, None]
    following = jnp.roll(keys, -1, axis=1)
    return jnp.where(position % 16 == 13, 0.985 * following, keys)


def student_pairs(key):
    inner = jax.random.fold_in(key, 21)
    scale = (SDIM // 4) ** (-0.5)
    return jax.random.truncated_normal(inner, -4.0, 4.0, (SDIM, SKVH * HEAD), jnp.float32) * scale


def draw_teacher_keys(key, part):
    base = shared_keys(key)
    return base.astype(jnp.bfloat16)


def draw_teacher_queries(key, part):
    key = jax.random.fold_in(key, 7)
    queries = jax.random.truncated_normal(key, -5.0, 5.0, (N_DP, SEQ, TDIM), jnp.float32)
    return queries.astype(jnp.bfloat16)


def draw_key_weight(key, part):
    base = student_pairs(key)
    return base.astype(jnp.bfloat16)


def draw_query_weight(key, part):
    key = jax.random.fold_in(key, 17)
    scale = (SDIM // 4) ** (-0.5)
    weights = jax.random.truncated_normal(key, -4.0, 4.0, (SDIM, SDIM), jnp.float32) * scale
    return weights.astype(jnp.bfloat16)


def draw_student_inputs(key, part):
    key = jax.random.fold_in(key, 9)
    normal_key, order_key = jax.random.split(key, 2)
    rows = jax.random.truncated_normal(normal_key, -4.0, 4.0, (N_DP, SEQ, SDIM), jnp.float32)
    paired = jax.random.permutation(order_key, N_DP)
    block = jnp.arange(SDIM) // (SDIM // N_DP)
    spike = jnp.where(block[None, None, :] == paired[:, None, None], 3.0, 1.0)
    rows = rows * spike
    return rows.astype(jnp.bfloat16)


def level_of(key, dims, shards, smallest, largest):
    loudness, own = 1.0, jax.random.fold_in(key, 6)
    for dim, shards_of in shards:
        draws = jnp.exp(jax.random.uniform(jax.random.fold_in(own, dim), (shards_of,), jnp.float32, smallest / len(shards), largest / len(shards)))
        loudness = loudness * jnp.repeat(draws, dims[dim] // shards_of).reshape([-1 if axis == dim else 1 for axis in range(len(dims))])
    return loudness


def normal_values(own_key, dims, scale, bound, cuts=(), dtype=jnp.bfloat16):
    loudness = level_of(own_key, dims, cuts, -0.22, 0.18) if cuts else 1.0
    values = jax.random.normal(own_key, dims, jnp.float32) * scale * loudness
    return jnp.minimum(jnp.maximum(values, -bound), bound).astype(dtype)


def setup_inputs(seed: int = 0) -> dict:
    seeds = jax.random.split(jax.random.key(seed), 9)
    teacher_queries = draw_teacher_queries(jax.random.fold_in(seeds[8], 71), 0)
    teacher_keys = draw_teacher_keys(jax.random.fold_in(seeds[8], 71), 0)
    teacher_values = normal_values(seeds[2], (N_DP, SEQ, TKVH * HEAD), 1.0, 6.0, ((0, 16), (2, 8)))
    projector = normal_values(seeds[3], (TDIM, SDIM), (TDIM // 16) ** -0.5, 0.25, ((0, 8),))
    student_inputs = draw_student_inputs(jax.random.fold_in(seeds[8], 71), 0)
    query_weight = draw_query_weight(jax.random.fold_in(seeds[8], 71), 0)
    key_weight = draw_key_weight(jax.random.fold_in(seeds[8], 71), 0)
    value_weight = normal_values(seeds[7], (SDIM, SKVH * HEAD), SDIM ** -0.5, 0.09375, ((0, 16), (1, 8)))
    return dict(teacher_queries=teacher_queries, teacher_keys=teacher_keys, teacher_values=teacher_values, projector=projector, student_inputs=student_inputs, query_weight=query_weight, key_weight=key_weight, value_weight=value_weight)


def attend(queries, keys, values, groups, factor):
    length = queries.shape[0]
    heads_kv = keys.shape[1] // HEAD
    query_heads = queries.astype(jnp.float32).reshape(length, heads_kv, groups, HEAD)
    key_heads = keys.astype(jnp.float32).reshape(length, heads_kv, HEAD)
    value_heads = values.astype(jnp.float32).reshape(length, heads_kv, HEAD)
    block_rows = min(512, length)
    pieces = []
    kept = []
    for number in range(length // block_rows):
        first = number * block_rows
        limit = first + block_rows
        scores = jnp.einsum("qhgd,khd->hgqk", query_heads[first:limit], key_heads[:limit]) * factor
        visible = jnp.arange(limit)[None, :] <= (first + jnp.arange(block_rows))[:, None]
        scores = jnp.where(visible, scores, -1e30)
        shifted = jnp.exp(scores - jnp.max(scores, axis=-1, keepdims=True))
        probs = shifted / jnp.sum(shifted, axis=-1, keepdims=True)
        rounded = lax.optimization_barrier(probs.astype(jnp.bfloat16)).astype(jnp.float32)
        context = jnp.einsum("hgqk,khd->qhgd", rounded, value_heads[:limit])
        pieces.append(context.reshape(block_rows, -1))
        kept.append(probs)
    return jnp.concatenate(pieces, axis=0), kept


def attend_back(incoming_all, queries, keys, values, kept, groups, factor):
    length = queries.shape[0]
    heads_kv = keys.shape[1] // HEAD
    query_heads = queries.astype(jnp.float32).reshape(length, heads_kv, groups, HEAD)
    key_heads = keys.astype(jnp.float32).reshape(length, heads_kv, HEAD)
    value_heads = values.astype(jnp.float32).reshape(length, heads_kv, HEAD)
    block_rows = min(512, length)
    grad_keys = jnp.zeros((length, heads_kv, HEAD), jnp.float32)
    grad_values = jnp.zeros((length, heads_kv, HEAD), jnp.float32)
    query_parts = []
    for number in range(length // block_rows):
        first = number * block_rows
        limit = first + block_rows
        probs = kept[number]
        rounded = lax.optimization_barrier(probs.astype(jnp.bfloat16)).astype(jnp.float32)
        incoming = incoming_all[first:limit].astype(jnp.float32).reshape(block_rows, heads_kv, groups, HEAD)
        grad_values = grad_values.at[:limit].add(jnp.einsum("hgqk,qhgd->khd", rounded, incoming))
        grad_probs = jnp.einsum("qhgd,khd->hgqk", incoming, value_heads[:limit])
        grad_scores = probs * (grad_probs - jnp.sum(grad_probs * probs, axis=-1, keepdims=True))
        scaled = lax.optimization_barrier((grad_scores * factor).astype(jnp.bfloat16)).astype(jnp.float32)
        query_parts.append(jnp.einsum("hgqk,khd->qhgd", scaled, key_heads[:limit]).reshape(block_rows, -1))
        grad_keys = grad_keys.at[:limit].add(jnp.einsum("hgqk,qhgd->khd", scaled, query_heads[first:limit]))
    grad_queries = jnp.concatenate(query_parts, axis=0).astype(jnp.bfloat16)
    return grad_queries, grad_keys.reshape(length, -1).astype(jnp.bfloat16), grad_values.reshape(length, -1).astype(jnp.bfloat16)


def reference(teacher_queries, teacher_keys, teacher_values, projector, student_inputs, query_weight, key_weight, value_weight):
    factor = HEAD ** -0.5
    width = TDIM // N_TENSOR
    weights = jnp.concatenate([query_weight, key_weight, value_weight], axis=1)
    kv_cols = SKVH * HEAD

    def one_sequence(carry, number):
        context_t, unused = attend(teacher_queries[number], teacher_keys[number], teacher_values[number], TQH // TKVH, factor)
        context_t = context_t.astype(jnp.bfloat16)
        target = jnp.zeros((SEQ, SDIM), jnp.float32)
        for block in range(N_TENSOR):
            partial_sum = jnp.dot(context_t[:, block * width:(block + 1) * width], projector[block * width:(block + 1) * width], preferred_element_type=jnp.float32)
            target = target + lax.optimization_barrier(partial_sum.astype(jnp.bfloat16)).astype(jnp.float32)
        inputs = student_inputs[number]
        projected = jnp.dot(inputs, weights, preferred_element_type=jnp.float32).astype(jnp.bfloat16)
        queries = projected[:, :SDIM]
        keys = projected[:, SDIM:SDIM + kv_cols]
        values = projected[:, SDIM + kv_cols:]
        context_s, kept = attend(queries, keys, values, SQH // SKVH, factor)
        grad_context = ((context_s - target) / N_DP).astype(jnp.bfloat16)
        grad_q, grad_k, grad_v = attend_back(grad_context, queries, keys, values, kept, SQH // SKVH, factor)
        grad_all = jnp.concatenate([grad_q, grad_k, grad_v], axis=1)
        term = jnp.dot(inputs.astype(jnp.float32).T, grad_all.astype(jnp.float32))
        return carry + term, 0

    start = jnp.zeros((SDIM, SDIM + 2 * kv_cols), jnp.float32)
    total, unused = lax.scan(one_sequence, start, jnp.arange(N_DP))
    return total[:, :SDIM], total[:, SDIM:SDIM + kv_cols], total[:, SDIM + kv_cols:]
```

```python
import jax
import jax.numpy as jnp
from jax import lax
from jax.sharding import Mesh, PartitionSpec as P

HEAD = 128
TQH = 64
TKVH = 8
SQH = 32
SKVH = 8
DP = ("ylo", "z", "core")
TENSOR = ("x", "yhi")


def attend(queries, keys, values, groups, factor):
    length = queries.shape[0]
    heads_kv = keys.shape[1] // HEAD
    query_heads = queries.reshape(length, heads_kv, groups, HEAD)
    key_heads = keys.reshape(length, heads_kv, HEAD)
    value_heads = values.reshape(length, heads_kv, HEAD)
    block_rows = min(512, length)
    pieces = []
    kept = []
    for number in range(length // block_rows):
        first = number * block_rows
        limit = first + block_rows
        scores = (
            jnp.einsum(
                "qhgd,khd->hgqk",
                query_heads[first:limit],
                key_heads[:limit],
                preferred_element_type=jnp.float32,
            )
            * factor
        )
        visible = jnp.arange(limit)[None, :] <= (first + jnp.arange(block_rows))[:, None]
        scores = jnp.where(visible, scores, -1e30)
        shifted = jnp.exp(scores - jnp.max(scores, axis=-1, keepdims=True))
        probs = shifted / jnp.sum(shifted, axis=-1, keepdims=True)
        rounded = probs.astype(jnp.bfloat16)
        context = jnp.einsum(
            "hgqk,khd->qhgd", rounded, value_heads[:limit], preferred_element_type=jnp.float32
        )
        pieces.append(context.reshape(block_rows, -1))
        kept.append(probs)
    return (jnp.concatenate(pieces, axis=0), kept)


def attend_back(incoming_all, queries, keys, values, kept, groups, factor):
    length = queries.shape[0]
    heads_kv = keys.shape[1] // HEAD
    query_heads = queries.reshape(length, heads_kv, groups, HEAD)
    key_heads = keys.reshape(length, heads_kv, HEAD)
    value_heads = values.reshape(length, heads_kv, HEAD)
    block_rows = min(512, length)
    grad_keys = jnp.zeros((length, heads_kv, HEAD), jnp.float32)
    grad_values = jnp.zeros((length, heads_kv, HEAD), jnp.float32)
    query_parts = []
    for number in range(length // block_rows):
        first = number * block_rows
        limit = first + block_rows
        probs = kept[number]
        rounded = probs.astype(jnp.bfloat16)
        incoming = incoming_all[first:limit].reshape(block_rows, heads_kv, groups, HEAD)
        grad_values = grad_values.at[:limit].add(
            jnp.einsum("hgqk,qhgd->khd", rounded, incoming, preferred_element_type=jnp.float32)
        )
        grad_probs = jnp.einsum(
            "qhgd,khd->hgqk", incoming, value_heads[:limit], preferred_element_type=jnp.float32
        )
        grad_scores = probs * (grad_probs - jnp.sum(grad_probs * probs, axis=-1, keepdims=True))
        scaled = (grad_scores * factor).astype(jnp.bfloat16)
        query_parts.append(
            jnp.einsum(
                "hgqk,khd->qhgd", scaled, key_heads[:limit], preferred_element_type=jnp.float32
            ).reshape(block_rows, -1)
        )
        grad_keys = grad_keys.at[:limit].add(
            jnp.einsum(
                "hgqk,qhgd->khd",
                scaled,
                query_heads[first:limit],
                preferred_element_type=jnp.float32,
            )
        )
    grad_queries = jnp.concatenate(query_parts, axis=0).astype(jnp.bfloat16)
    return grad_queries, grad_keys.reshape(length, -1), grad_values.reshape(length, -1)


def shift(array, axis, step):
    n = lax.axis_size(axis)
    return lax.ppermute(array, axis, [(i, (i + step) % n) for i in range(n)])


def gather_rows(own):
    rows, width = own.shape
    half = rows // 2
    x = lax.axis_index("x")
    y = lax.axis_index("yhi")
    buffer = jnp.zeros((8 * rows, width), own.dtype)

    def place(buffer, piece, dx, side, offset=0):
        at = (((x + dx) % 4) * 2 + side) * rows + offset
        return lax.dynamic_update_slice(buffer, piece, (at, 0))

    other = shift(own, "yhi", 1)
    buffer = place(buffer, own, 0, y)
    for block, side in ((own, y), (other, 1 - y)):
        left = shift(block, "x", 1)
        right = shift(block, "x", -1)
        far_top = shift(left[:half], "x", 1)
        far_bottom = shift(right[half:], "x", -1)
        if block is other:
            buffer = place(buffer, other, 0, side)
        buffer = place(buffer, left, 3, side)
        buffer = place(buffer, right, 1, side)
        buffer = place(buffer, far_top, 2, side)
        buffer = place(buffer, far_bottom, 2, side, half)
    return buffer


def reduce_target(part):
    summed = lax.psum_scatter(part, "x", scatter_dimension=0, tiled=True)
    width = summed.shape[0] // 2
    y = lax.axis_index("yhi")
    theirs = lax.dynamic_slice_in_dim(summed, (1 - y) * width, width, 0)
    mine = lax.dynamic_slice_in_dim(summed, y * width, width, 0)
    return mine.astype(jnp.float32) + shift(theirs, "yhi", 1).astype(jnp.float32)


def reduce_grads(whole):
    cols = whole.shape[1]
    parts = whole.astype(jnp.bfloat16).reshape(8, 2, 256, cols)
    c = lax.axis_index("core")
    y = lax.axis_index("ylo")
    theirs = lax.dynamic_index_in_dim(parts, 1 - c, 1, keepdims=False)
    mine = lax.dynamic_index_in_dim(parts, c, 1, keepdims=False)
    pair = (mine.astype(jnp.float32) + shift(theirs, "core", 1).astype(jnp.float32)).astype(
        jnp.bfloat16
    )
    pair = pair.reshape(2, 4, 256, cols).transpose(1, 0, 2, 3).reshape(4, 512, cols)
    summed = lax.psum_scatter(pair, "z", scatter_dimension=0, tiled=True).reshape(512, cols)
    theirs = lax.dynamic_slice_in_dim(summed, (1 - y) * 256, 256, 0)
    mine = lax.dynamic_slice_in_dim(summed, y * 256, 256, 0)
    return mine.astype(jnp.float32) + shift(theirs, "ylo", 1).astype(jnp.float32)


def per_device(
    teacher_queries,
    teacher_keys,
    teacher_values,
    projector,
    student_inputs,
    query_weight,
    key_weight,
    value_weight,
):
    factor = HEAD ** (-0.5)
    dp_count = 16
    weights = lax.all_gather(
        jnp.concatenate([query_weight, key_weight, value_weight], axis=1), DP, axis=0, tiled=True
    )
    rows_all = gather_rows(student_inputs[0])

    context_t, unused = attend(
        teacher_queries[0], teacher_keys[0], teacher_values[0], TQH // TKVH, factor
    )
    context_t = context_t.astype(jnp.bfloat16)
    split = projector.reshape(projector.shape[0], 8, 2, 256)
    targets = []
    for j in range(2):
        part = lax.dot_general(
            split[:, :, j].reshape(-1, 2048),
            context_t,
            (((0,), (1,)), ((), ())),
            preferred_element_type=jnp.float32,
        ).astype(jnp.bfloat16)
        targets.append(reduce_target(part))

    projected = jnp.dot(rows_all, weights, preferred_element_type=jnp.float32).astype(jnp.bfloat16)
    queries = projected[:, :512]
    keys = projected[:, 512:640]
    values = projected[:, 640:]
    context_s, kept = attend(queries, keys, values, SQH // SKVH, factor)

    grad_k = grad_v = 0.0
    reduced = []
    for j in range(2):
        cols = slice(j * 256, j * 256 + 256)
        grad_context = ((context_s[:, cols] - targets[j].T) / dp_count).astype(jnp.bfloat16)
        grad_q, more_k, more_v = attend_back(
            grad_context,
            queries[:, cols],
            keys,
            values,
            [probs[:, 2 * j : 2 * j + 2] for probs in kept],
            2,
            factor,
        )
        grad_k += more_k
        grad_v += more_v
        reduced.append(
            reduce_grads(
                lax.dot_general(
                    rows_all, grad_q, (((0,), (0,)), ((), ())), preferred_element_type=jnp.float32
                )
            )
        )
    grad_kv = jnp.concatenate([grad_k, grad_v], axis=1).astype(jnp.bfloat16)
    last = reduce_grads(
        lax.dot_general(
            rows_all, grad_kv, (((0,), (0,)), ((), ())), preferred_element_type=jnp.float32
        )
    )
    return jnp.concatenate(reduced, axis=1), last[:, :128], last[:, 128:]


def solution(mesh):
    fine = Mesh(mesh.devices.reshape(2, 4, 2, 4, 2), DP + TENSOR)
    placed = (
        P(DP, None, TENSOR),
        P(DP, None, TENSOR),
        P(DP, None, TENSOR),
        P(TENSOR, None),
        P(DP, TENSOR, None),
        P(DP, TENSOR),
        P(DP, TENSOR),
        P(DP, TENSOR),
    )
    return jax.shard_map(
        per_device,
        mesh=fine,
        in_specs=placed,
        out_specs=(P(DP, TENSOR), P(DP, TENSOR), P(DP, TENSOR)),
        check_vma=False,
    )
```

```python
import jax
import jax.numpy as jnp
from jax import lax
from jax.experimental import pallas as pl
from jax.experimental.pallas import tpu as pltpu
from jax.sharding import Mesh, PartitionSpec as P

HEAD = 128
FACTOR = HEAD ** (-0.5)
LOG2E = 1.4426950408889634
BLOCK = 256
SEQ = 1024
DP = ("ylo", "z", "core")
TENSOR = ("x", "yhi")
NT = (((1,), (1,)), ((), ()))
VMEM = pltpu.CompilerParams(vmem_limit_bytes=48 * 1024 * 1024)


def dot(a, b):
    return jnp.dot(a, b, preferred_element_type=jnp.float32)


def teacher_kernel(q_ref, k_ref, v_ref, o_ref):
    for number in range(SEQ // BLOCK):
        first = number * BLOCK
        limit = first + BLOCK
        scores = lax.dot_general(
            q_ref[first:limit, :], k_ref[:limit, :], NT, preferred_element_type=jnp.float32
        )
        row = first + lax.broadcasted_iota(jnp.int32, scores.shape, 0)
        col = lax.broadcasted_iota(jnp.int32, scores.shape, 1)
        scores = jnp.where(col <= row, scores, -1e30)
        top = jnp.max(scores, axis=1, keepdims=True)
        weights = jnp.exp2((scores - top) * (FACTOR * LOG2E))
        total = jnp.sum(weights, axis=1, keepdims=True)
        context = dot(weights.astype(jnp.bfloat16), v_ref[:limit, :])
        o_ref[first:limit, :] = (context / total).astype(jnp.bfloat16)


def teacher_attention(queries, keys, values, first, count):
    return pl.pallas_call(
        teacher_kernel,
        grid=(count,),
        in_specs=[
            pl.BlockSpec((SEQ, HEAD), lambda h: (0, first + h)),
            pl.BlockSpec((SEQ, HEAD), lambda h: (0, 0)),
            pl.BlockSpec((SEQ, HEAD), lambda h: (0, 0)),
        ],
        out_specs=pl.BlockSpec((SEQ, HEAD), lambda h: (0, h)),
        out_shape=jax.ShapeDtypeStruct((SEQ, count * HEAD), jnp.bfloat16),
        compiler_params=VMEM,
        name="teacher_attention",
    )(queries, keys, values)


def project_kernel(a_ref, b_ref, p_ref, o_ref):
    half = a_ref.shape[1]
    o_ref[0] = (dot(a_ref[...], p_ref[:half, :]) + dot(b_ref[...], p_ref[half:, :])).astype(
        jnp.bfloat16
    )


def project(context_a, context_b, projector, part):
    rows = projector.shape[0]
    return pl.pallas_call(
        project_kernel,
        grid=(8,),
        in_specs=[
            pl.BlockSpec(context_a.shape, lambda g: (0, 0)),
            pl.BlockSpec(context_b.shape, lambda g: (0, 0)),
            pl.BlockSpec((rows, 256), lambda g: (0, 2 * g + part)),
        ],
        out_specs=pl.BlockSpec((1, SEQ, 256), lambda g: (g, 0, 0)),
        out_shape=jax.ShapeDtypeStruct((8, SEQ, 256), jnp.bfloat16),
        compiler_params=VMEM,
        name="project",
    )(context_a, context_b, projector)


def student_kernel(has_start, y_ref, q_ref, k_ref, v_ref, mine_ref, theirs_ref, *rest):
    if has_start:
        start_ref, gq_ref, gkv_ref, kt, vt, dk, dv = rest
    else:
        gq_ref, gkv_ref, kt, vt, dk, dv = rest
    step = pl.program_id(0)

    @pl.when(step == 0)
    def _():
        kt[...] = k_ref[...].T
        vt[...] = v_ref[...].T
        if has_start:
            dk[...] = start_ref[:, :HEAD]
            dv[...] = start_ref[:, HEAD:]
        else:
            dk[...] = jnp.zeros_like(dk)
            dv[...] = jnp.zeros_like(dv)

    for number in range(SEQ // BLOCK):
        first = number * BLOCK
        limit = first + BLOCK
        queries = q_ref[first:limit, :]
        scores = lax.dot_general(k_ref[:limit, :], queries, NT, preferred_element_type=jnp.float32)
        key = lax.broadcasted_iota(jnp.int32, scores.shape, 0)
        query = first + lax.broadcasted_iota(jnp.int32, scores.shape, 1)
        scores = jnp.where(key <= query, scores, -1e30)
        top = jnp.max(scores, axis=0, keepdims=True)
        weights = jnp.exp2((scores - top) * (FACTOR * LOG2E))
        probs = weights * (1.0 / jnp.sum(weights, axis=0, keepdims=True))
        rounded = probs.astype(jnp.bfloat16)
        context = dot(vt[:, :limit], rounded).T
        target = mine_ref[0, first:limit, :].astype(jnp.float32) + theirs_ref[
            first:limit, :
        ].astype(jnp.float32)
        incoming = ((context - target) * (1.0 / 16)).astype(jnp.bfloat16)
        grad_probs = lax.dot_general(
            v_ref[:limit, :], incoming, NT, preferred_element_type=jnp.float32
        )
        inner = jnp.sum(grad_probs * probs, axis=0, keepdims=True)
        scaled = (probs * (grad_probs - inner) * FACTOR).astype(jnp.bfloat16)
        dv[:limit, :] += dot(rounded, incoming)
        dk[:limit, :] += dot(scaled, queries)
        gq_ref[first:limit, :] = dot(kt[:, :limit], scaled).T.astype(jnp.bfloat16)

    @pl.when(step == pl.num_programs(0) - 1)
    def _():
        gkv_ref[:, :HEAD] = dk[...].astype(gkv_ref.dtype)
        gkv_ref[:, HEAD:] = dv[...].astype(gkv_ref.dtype)


def student_attention(y, projected, mine, theirs, part, start=None):
    specs = [
        pl.BlockSpec((SEQ, HEAD), lambda h, y: (0, 2 * part + h)),
        pl.BlockSpec((SEQ, HEAD), lambda h, y: (0, 4)),
        pl.BlockSpec((SEQ, HEAD), lambda h, y: (0, 5)),
        pl.BlockSpec((1, SEQ, HEAD), lambda h, y: (y[0], 0, h)),
        pl.BlockSpec((SEQ, HEAD), lambda h, y: (0, h)),
    ]
    operands = [projected, projected, projected, mine, theirs]
    if start is not None:
        specs.append(pl.BlockSpec((SEQ, 2 * HEAD), lambda h, y: (0, 0)))
        operands.append(start)
    return pl.pallas_call(
        lambda *refs: student_kernel(start is not None, *refs),
        grid_spec=pltpu.PrefetchScalarGridSpec(
            num_scalar_prefetch=1,
            grid=(2,),
            in_specs=specs,
            out_specs=[
                pl.BlockSpec((SEQ, HEAD), lambda h, y: (0, h)),
                pl.BlockSpec((SEQ, 2 * HEAD), lambda h, y: (0, 0)),
            ],
            scratch_shapes=[
                pltpu.VMEM((HEAD, SEQ), jnp.bfloat16),
                pltpu.VMEM((HEAD, SEQ), jnp.bfloat16),
                pltpu.VMEM((SEQ, HEAD), jnp.float32),
                pltpu.VMEM((SEQ, HEAD), jnp.float32),
            ],
        ),
        out_shape=[
            jax.ShapeDtypeStruct((SEQ, 2 * HEAD), jnp.bfloat16),
            jax.ShapeDtypeStruct(
                (SEQ, 2 * HEAD), jnp.float32 if start is None else jnp.bfloat16
            ),
        ],
        compiler_params=VMEM,
        name="student_attention",
    )(y, *operands)


def shift(array, axis, step=1):
    n = lax.axis_size(axis)
    return lax.ppermute(array, axis, [(i, (i + step) % n) for i in range(n)])


def swap_core(whole):
    parts = whole.astype(jnp.bfloat16).reshape(8, 2, 256, whole.shape[1])
    c = lax.axis_index("core")
    theirs = lax.dynamic_index_in_dim(parts, 1 - c, 1, keepdims=False)
    mine = lax.dynamic_index_in_dim(parts, c, 1, keepdims=False)
    return mine.astype(jnp.float32) + shift(theirs, "core").astype(jnp.float32)


def reduce_ring(whole):
    cols = whole.shape[1]
    pair = swap_core(whole).astype(jnp.bfloat16)
    pair = pair.reshape(2, 4, 256, cols).transpose(1, 0, 2, 3).reshape(4, 512, cols)
    summed = lax.psum_scatter(pair, "z", scatter_dimension=0, tiled=True).reshape(2, 256, cols)
    y = lax.axis_index("ylo")
    theirs = lax.dynamic_index_in_dim(summed, 1 - y, 0, keepdims=False)
    mine = lax.dynamic_index_in_dim(summed, y, 0, keepdims=False)
    return mine.astype(jnp.float32) + shift(theirs, "ylo").astype(jnp.float32)


def reduce_direct(whole):
    pair = swap_core(whole).astype(jnp.bfloat16)
    y = lax.axis_index("ylo")
    z = lax.axis_index("z")
    total = lax.dynamic_index_in_dim(pair, y * 4 + z, 0, keepdims=False).astype(jnp.float32)
    for dy in range(2):
        for dz in range(4):
            if dy or dz:
                there = (y + dy) % 2 * 4 + (z + dz) % 4
                route = [
                    (i * 4 + k, (i + dy) % 2 * 4 + (k + dz) % 4) for i in range(2) for k in range(4)
                ]
                sent = lax.dynamic_index_in_dim(pair, there, 0, keepdims=False)
                total += lax.ppermute(sent, ("ylo", "z"), route).astype(jnp.float32)
    return total


def per_device(
    teacher_queries,
    teacher_keys,
    teacher_values,
    projector,
    student_inputs,
    query_weight,
    key_weight,
    value_weight,
):
    tq, tk, tv = teacher_queries[0], teacher_keys[0], teacher_values[0]
    yhi = lax.axis_index("yhi")
    own = student_inputs[0]
    weights = lax.all_gather(
        jnp.concatenate([query_weight, key_weight, value_weight], axis=1), DP, axis=0, tiled=True
    )
    other = shift(own, "yhi")
    own_all = lax.all_gather(own, "x", axis=0, tiled=True)
    other_all = lax.all_gather(other, "x", axis=0, tiled=True)

    context_a = teacher_attention(tq, tk, tv, 0, 4)
    tq, other = lax.optimization_barrier((tq, other))
    context_b = teacher_attention(tq, tk, tv, 4, 4)
    context_b, own_all, weights = lax.optimization_barrier((context_b, own_all, weights))
    sums = []
    for part in range(2):
        product = project(context_a, context_b, projector, part)
        sums.append(
            lax.psum_scatter(product, "x", scatter_dimension=0, tiled=True)
        )

    pieces = jnp.stack([own_all.reshape(4, 128, -1), other_all.reshape(4, 128, -1)], axis=1)
    flipped = jnp.stack([other_all.reshape(4, 128, -1), own_all.reshape(4, 128, -1)], axis=1)
    rows_all = jnp.where(yhi == 0, pieces, flipped).reshape(SEQ, -1)
    projected = dot(rows_all, weights).astype(jnp.bfloat16)

    y = yhi.astype(jnp.int32).reshape(1)
    theirs = [
        shift(lax.dynamic_index_in_dim(s, 1 - yhi, 0, keepdims=False), "yhi") for s in sums
    ]
    across = (((0,), (0,)), ((), ()))
    grad_a, part_kv = student_attention(y, projected, sums[0], theirs[0], 0)
    out_a = reduce_ring(
        lax.dot_general(rows_all, grad_a, across, preferred_element_type=jnp.float32)
    )
    grad_b, grad_kv = student_attention(y, projected, sums[1], theirs[1], 1, part_kv)
    out_b = reduce_direct(
        lax.dot_general(
            rows_all,
            jnp.concatenate([grad_b, grad_kv], axis=1),
            across,
            preferred_element_type=jnp.float32,
        )
    )
    return jnp.concatenate([out_a, out_b[:, :256]], axis=1), out_b[:, 256:384], out_b[:, 384:]


def solution(mesh):
    fine = Mesh(mesh.devices.reshape(2, 4, 2, 4, 2), DP + TENSOR)
    placed = (
        P(DP, None, TENSOR),
        P(DP, None, TENSOR),
        P(DP, None, TENSOR),
        P(TENSOR, None),
        P(DP, TENSOR, None),
        P(DP, TENSOR),
        P(DP, TENSOR),
        P(DP, TENSOR),
    )
    return jax.shard_map(
        per_device,
        mesh=fine,
        in_specs=placed,
        out_specs=(P(DP, TENSOR), P(DP, TENSOR), P(DP, TENSOR)),
        check_vma=False,
    )
```

```python
import jax
import jax.numpy as jnp
from jax import lax
from jax.experimental import pallas as pl
from jax.experimental.pallas import tpu as pltpu
from jax.sharding import Mesh, PartitionSpec as P

HEAD = 128
FACTOR = HEAD ** (-0.5)
LOG2E = 1.4426950408889634
BLOCK = 256
SEQ = 1024
DP = ("ylo", "z", "core")
TENSOR = ("x", "yhi")
NT = (((1,), (1,)), ((), ()))
VMEM = pltpu.CompilerParams(vmem_limit_bytes=48 * 1024 * 1024)


def cost(us, moved=0):
    return pl.CostEstimate(flops=int(us * 1.0e9), bytes_accessed=moved, transcendentals=0)


def dot(a, b):
    return jnp.dot(a, b, preferred_element_type=jnp.float32)


def teacher_kernel(q_ref, k_ref, v_ref, o_ref):
    for number in range(SEQ // BLOCK):
        first = number * BLOCK
        limit = first + BLOCK
        scores = lax.dot_general(
            q_ref[first:limit, :], k_ref[:limit, :], NT, preferred_element_type=jnp.float32
        )
        row = lax.broadcasted_iota(jnp.int32, (BLOCK, BLOCK), 0)
        col = lax.broadcasted_iota(jnp.int32, (BLOCK, BLOCK), 1)
        last = jnp.where(col <= row, scores[:, first:], -1e30)
        scores = jnp.concatenate([scores[:, :first], last], axis=1) if first else last
        top = jnp.max(scores, axis=1, keepdims=True)
        weights = jnp.exp2((scores - top) * (FACTOR * LOG2E))
        total = jnp.sum(weights, axis=1, keepdims=True)
        context = dot(weights.astype(jnp.bfloat16), v_ref[:limit, :])
        o_ref[first:limit, :] = (context / total).astype(jnp.bfloat16)


def teacher_attention(queries, keys, values, first, count):
    return pl.pallas_call(
        teacher_kernel,
        grid=(count,),
        in_specs=[
            pl.BlockSpec((SEQ, HEAD), lambda h: (0, first + h)),
            pl.BlockSpec((SEQ, HEAD), lambda h: (0, 0)),
            pl.BlockSpec((SEQ, HEAD), lambda h: (0, 0)),
        ],
        out_specs=pl.BlockSpec((SEQ, HEAD), lambda h: (0, h)),
        out_shape=jax.ShapeDtypeStruct((SEQ, count * HEAD), jnp.bfloat16),
        compiler_params=VMEM,
        cost_estimate=cost(7),
        name="teacher_attention",
    )(queries, keys, values)


def project_kernel(order_ref, a_ref, b_ref, p_ref, o_ref, context):
    half = a_ref.shape[1]

    @pl.when(pl.program_id(0) == 0)
    def _():
        context[:, :half] = a_ref[...]
        context[:, half:] = b_ref[...]

    o_ref[0] = dot(context[...], p_ref[...]).astype(jnp.bfloat16)


def project(order, context_a, context_b, projector):
    rows = projector.shape[0]
    count = order.shape[0]
    return pl.pallas_call(
        project_kernel,
        grid_spec=pltpu.PrefetchScalarGridSpec(
            num_scalar_prefetch=1,
            grid=(count,),
            in_specs=[
                pl.BlockSpec(context_a.shape, lambda g, order: (0, 0)),
                pl.BlockSpec(context_b.shape, lambda g, order: (0, 0)),
                pl.BlockSpec((rows, 256), lambda g, order: (0, order[g])),
            ],
            out_specs=pl.BlockSpec((1, SEQ, 256), lambda g, order: (g, 0, 0)),
            scratch_shapes=[pltpu.VMEM((SEQ, rows), jnp.bfloat16)],
        ),
        out_shape=jax.ShapeDtypeStruct((count, SEQ, 256), jnp.bfloat16),
        compiler_params=VMEM,
        cost_estimate=cost(count),
        name="project",
    )(order, context_a, context_b, projector)


def fill(scratch, piece_refs):
    at = 0
    for ref in piece_refs:
        scratch[at : at + ref.shape[0], :] = ref[...]
        at += ref.shape[0]


def student_project_kernel(*refs):
    at_ref, pieces, (w_ref, o_ref, left, total) = refs[0], refs[1:-4], refs[-4:]
    step = pl.program_id(0)
    fill(left, pieces)
    product = dot(left[...], w_ref[...])

    @pl.when(step == 0)
    def _():
        total[...] = product

    @pl.when(step > 0)
    def _():
        total[...] += product

    @pl.when(step == pl.num_programs(0) - 1)
    def _():
        first = 0
        for number, ref in enumerate(pieces):
            size = ref.shape[0]
            o_ref[pl.ds(pl.multiple_of(at_ref[number], 64), size), :] = total[
                first : first + size, :
            ].astype(jnp.bfloat16)
            first += size


def student_project(places, pieces, weights):
    depth, cols = weights.shape
    block = 1024
    return pl.pallas_call(
        student_project_kernel,
        grid_spec=pltpu.PrefetchScalarGridSpec(
            num_scalar_prefetch=1,
            grid=(depth // block,),
            in_specs=[pl.BlockSpec((p.shape[0], block), lambda k, at: (0, k)) for p in pieces]
            + [pl.BlockSpec((block, cols), lambda k, at: (k, 0))],
            out_specs=pl.BlockSpec((SEQ, cols), lambda k, at: (0, 0)),
            scratch_shapes=[
                pltpu.VMEM((SEQ, block), jnp.bfloat16),
                pltpu.VMEM((SEQ, cols), jnp.float32),
            ],
        ),
        out_shape=jax.ShapeDtypeStruct((SEQ, cols), jnp.bfloat16),
        compiler_params=VMEM,
        cost_estimate=cost(9),
        name="student_project",
    )(places, *pieces, weights)


def weight_grad_kernel(count, *refs):
    at_ref, grads, pieces = refs[0], refs[2 : 2 + count], refs[2 + count : -4]
    o_ref, left, right, across = refs[-4:]

    @pl.when(pl.program_id(0) == 0)
    def _():
        first = 0
        for number, ref in enumerate(pieces):
            size = ref.shape[0]
            col = 0
            for grad in grads:
                right[first : first + size, col : col + grad.shape[1]] = grad[
                    pl.ds(pl.multiple_of(at_ref[number], 64), size), :
                ]
                col += grad.shape[1]
            first += size
        across[...] = right[...].T

    fill(left, pieces)
    o_ref[0] = dot(across[...], left[...]).astype(jnp.bfloat16)


def weight_grad(places, blocks, grads, pieces):
    cols = sum(g.shape[1] for g in grads)
    return pl.pallas_call(
        lambda *refs: weight_grad_kernel(len(grads), *refs),
        grid_spec=pltpu.PrefetchScalarGridSpec(
            num_scalar_prefetch=2,
            grid=(8,),
            in_specs=[pl.BlockSpec(g.shape, lambda k, at, order: (0, 0)) for g in grads]
            + [
                pl.BlockSpec((p.shape[0], 256), lambda k, at, order: (0, order[k])) for p in pieces
            ],
            out_specs=pl.BlockSpec((1, cols, 256), lambda k, at, order: (k, 0, 0)),
            scratch_shapes=[
                pltpu.VMEM((SEQ, 256), jnp.bfloat16),
                pltpu.VMEM((SEQ, cols), jnp.bfloat16),
                pltpu.VMEM((cols, SEQ), jnp.bfloat16),
            ],
        ),
        out_shape=jax.ShapeDtypeStruct((8, cols, 256), jnp.bfloat16),
        compiler_params=VMEM,
        cost_estimate=cost(4),
        name="weight_grad",
    )(places, blocks, *grads, *pieces)


def pair_kernel(a_ref, b_ref, *outs):
    for number, ref in enumerate(outs):
        ref[...] = (
            a_ref[number].astype(jnp.float32) + b_ref[number].astype(jnp.float32)
        ).astype(jnp.bfloat16)


def pair_sum(a, b):
    return pl.pallas_call(
        pair_kernel,
        out_shape=[jax.ShapeDtypeStruct(a.shape[1:], jnp.bfloat16) for _ in range(a.shape[0])],
        compiler_params=VMEM,
        cost_estimate=cost(3),
        name="pair_sum",
    )(a, b)


def student_kernel(has_start, y_ref, q_ref, k_ref, v_ref, mine_ref, *rest):
    if has_start:
        start_ref, gq_ref, gkv_ref, kt, vt, dk, dv = rest
    else:
        theirs_ref, gq_ref, gkv_ref, kt, vt, dk, dv = rest
    step = pl.program_id(0)

    @pl.when(step == 0)
    def _():
        kt[...] = k_ref[...].T
        vt[...] = v_ref[...].T
        if has_start:
            dk[...] = start_ref[:, :HEAD]
            dv[...] = start_ref[:, HEAD:]
        else:
            dk[...] = jnp.zeros_like(dk)
            dv[...] = jnp.zeros_like(dv)

    for number in range(SEQ // BLOCK):
        first = number * BLOCK
        limit = first + BLOCK
        queries = q_ref[first:limit, :]
        scores = lax.dot_general(k_ref[:limit, :], queries, NT, preferred_element_type=jnp.float32)
        key = lax.broadcasted_iota(jnp.int32, (BLOCK, BLOCK), 0)
        query = lax.broadcasted_iota(jnp.int32, (BLOCK, BLOCK), 1)
        last = jnp.where(key <= query, scores[first:], -1e30)
        scores = jnp.concatenate([scores[:first], last], axis=0) if first else last
        top = jnp.max(scores, axis=0, keepdims=True)
        weights = jnp.exp2((scores - top) * (FACTOR * LOG2E))
        probs = weights * (1.0 / jnp.sum(weights, axis=0, keepdims=True))
        rounded = probs.astype(jnp.bfloat16)
        context = dot(vt[:, :limit], rounded).T
        target = mine_ref[0, first:limit, :].astype(jnp.float32)
        if not has_start:
            target += theirs_ref[first:limit, :].astype(jnp.float32)
        incoming = ((context - target) * (1.0 / 16)).astype(jnp.bfloat16)
        grad_probs = lax.dot_general(
            v_ref[:limit, :], incoming, NT, preferred_element_type=jnp.float32
        )
        inner = jnp.sum(grad_probs * probs, axis=0, keepdims=True)
        scaled = (probs * (grad_probs - inner)).astype(jnp.bfloat16)
        dv[:limit, :] += dot(rounded, incoming)
        dk[:limit, :] += dot(scaled, queries)
        gq_ref[first:limit, :] = (dot(kt[:, :limit], scaled) * FACTOR).T.astype(jnp.bfloat16)

    @pl.when(step == pl.num_programs(0) - 1)
    def _():
        keys_scale = 1.0 if gkv_ref.dtype == jnp.float32 else FACTOR
        gkv_ref[:, :HEAD] = (dk[...] * keys_scale).astype(gkv_ref.dtype)
        gkv_ref[:, HEAD:] = dv[...].astype(gkv_ref.dtype)


def student_attention(y, projected, mine, part, theirs=None, start=None):
    specs = [
        pl.BlockSpec((SEQ, HEAD), lambda h, y: (0, 2 * part + h)),
        pl.BlockSpec((SEQ, HEAD), lambda h, y: (0, 4)),
        pl.BlockSpec((SEQ, HEAD), lambda h, y: (0, 5)),
        pl.BlockSpec((1, SEQ, HEAD), lambda h, y: (y[0], 0, h)),
    ]
    operands = [projected, projected, projected, mine]
    if theirs is not None:
        specs.append(pl.BlockSpec((SEQ, HEAD), lambda h, y: (0, h)))
        operands.append(theirs)
    if start is not None:
        specs.append(pl.BlockSpec((SEQ, 2 * HEAD), lambda h, y: (0, 0)))
        operands.append(start)
    return pl.pallas_call(
        lambda *refs: student_kernel(start is not None, *refs),
        grid_spec=pltpu.PrefetchScalarGridSpec(
            num_scalar_prefetch=1,
            grid=(2,),
            in_specs=specs,
            out_specs=[
                pl.BlockSpec((SEQ, HEAD), lambda h, y: (0, h)),
                pl.BlockSpec((SEQ, 2 * HEAD), lambda h, y: (0, 0)),
            ],
            scratch_shapes=[
                pltpu.VMEM((HEAD, SEQ), jnp.bfloat16),
                pltpu.VMEM((HEAD, SEQ), jnp.bfloat16),
                pltpu.VMEM((SEQ, HEAD), jnp.float32),
                pltpu.VMEM((SEQ, HEAD), jnp.float32),
            ],
        ),
        out_shape=[
            jax.ShapeDtypeStruct((SEQ, 2 * HEAD), jnp.bfloat16),
            jax.ShapeDtypeStruct(
                (SEQ, 2 * HEAD), jnp.float32 if start is None else jnp.bfloat16
            ),
        ],
        compiler_params=VMEM,
        cost_estimate=cost(11),
        name="student_attention",
    )(y, *operands)


def shift(array, axis, step=1):
    n = lax.axis_size(axis)
    return lax.ppermute(array, axis, [(i, (i + step) % n) for i in range(n)])


def gather_rows_near(own):
    return shift(own, "yhi"), shift(own, "x", 1), shift(own, "x", -1)


def far_halves(left, right):
    half = left.shape[0] // 2
    return shift(left[:half], "x", 1), shift(right[half:], "x", -1)


def row_places(x, y):
    places = []
    for side in (y, 1 - y):
        for dx, offset in ((0, 0), (3, 0), (1, 0), (2, 0), (2, 64)):
            places.append((((x + dx) % 4) * 2 + side) * 128 + offset)
    return jnp.stack(places).astype(jnp.int32)


RELATIVE = [(dy, dz) for dy in range(2) for dz in range(4)]


def row_blocks(core):
    y = lax.axis_index("ylo")
    z = lax.axis_index("z")
    return jnp.stack(
        [(((y + dy) % 2) * 4 + (z + dz) % 4) * 2 + core for dy, dz in RELATIVE]
    ).astype(jnp.int32)


def send_direct(blocks):
    got = [blocks[0]]
    for (dy, dz), block in zip(RELATIVE[1:], blocks[1:]):
        route = [(i * 4 + k, (i + dy) % 2 * 4 + (k + dz) % 4) for i in range(2) for k in range(4)]
        got.append(lax.ppermute(block, ("ylo", "z"), route))
    return got


def finish_kernel(*refs):
    a_refs, b_refs, (q_ref, k_ref, v_ref) = refs[:8], refs[8:16], refs[16:]

    def total(parts):
        result = parts[0][...].astype(jnp.float32)
        for part in parts[1:]:
            result += part[...].astype(jnp.float32)
        return result.T

    q_ref[:, :256] = total(a_refs)
    rest = total(b_refs)
    q_ref[:, 256:] = rest[:, :256]
    k_ref[...] = rest[:, 256:384]
    v_ref[...] = rest[:, 384:]


def finish(got_a, got_b):
    return pl.pallas_call(
        finish_kernel,
        out_shape=[jax.ShapeDtypeStruct((256, cols), jnp.float32) for cols in (512, 128, 128)],
        compiler_params=VMEM,
        cost_estimate=cost(3),
        name="finish",
    )(*got_a, *got_b)


def per_device(
    teacher_queries,
    teacher_keys,
    teacher_values,
    projector,
    student_inputs,
    query_weight,
    key_weight,
    value_weight,
):
    tq, tk, tv = teacher_queries[0], teacher_keys[0], teacher_values[0]
    x = lax.axis_index("x")
    yhi = lax.axis_index("yhi")
    core = lax.axis_index("core")
    own = student_inputs[0]
    weights = lax.all_gather(
        jnp.concatenate([query_weight, key_weight, value_weight], axis=1), DP, axis=0, tiled=True
    )
    other, left, right = gather_rows_near(own)

    groups = jnp.arange(4, dtype=jnp.int32)
    context_a = teacher_attention(tq, tk, tv, 0, 4)
    context_b = teacher_attention(tq, tk, tv, 4, 4)
    far = far_halves(left, right)
    context_b, far, other, weights = lax.optimization_barrier((context_b, far, other, weights))

    other_left, other_right = shift(other, "x", 1), shift(other, "x", -1)

    product_a = project(2 * jnp.arange(8, dtype=jnp.int32), context_a, context_b, projector)
    sum_a = lax.psum_scatter(product_a, "x", scatter_dimension=0, tiled=True)

    sent = project(2 * (2 * groups + 1 - yhi) + 1, context_a, context_b, projector)
    came = shift(sent, "yhi")
    context_b, other_left, other_right = lax.optimization_barrier(
        (context_b, other_left, other_right)
    )
    kept = project(2 * (2 * groups + yhi) + 1, context_a, context_b, projector)

    other_far = far_halves(other_left, other_right)
    pieces = [own, left, right, *far, other, other_left, other_right, *other_far]
    places = row_places(x, yhi)
    projected = student_project(places, pieces, weights)

    both = (kept.astype(jnp.float32) + came.astype(jnp.float32)).astype(jnp.bfloat16)
    sum_b = lax.psum_scatter(both, "x", scatter_dimension=0, tiled=True)

    y = yhi.astype(jnp.int32).reshape(1)
    theirs_a = shift(lax.dynamic_index_in_dim(sum_a, 1 - yhi, 0, keepdims=False), "yhi")

    def reduced(grads):
        sent = weight_grad(places, row_blocks(1 - core), grads, pieces)
        kept = weight_grad(places, row_blocks(core), grads, pieces)
        return list(pair_sum(kept, shift(sent, "core")))

    grad_a, part_kv = student_attention(y, projected, sum_a, 0, theirs=theirs_a)
    blocks_a = reduced([grad_a])
    sum_b, blocks_a[0] = lax.optimization_barrier((sum_b, blocks_a[0]))
    got_a = send_direct(blocks_a)
    grad_b, grad_kv = student_attention(
        jnp.zeros((1,), jnp.int32), projected, sum_b, 1, start=part_kv
    )
    got_a, grad_b = lax.optimization_barrier((got_a, grad_b))
    got_b = send_direct(reduced([grad_b, grad_kv]))
    return tuple(finish(got_a, got_b))


def solution(mesh):
    fine = Mesh(mesh.devices.reshape(2, 4, 2, 4, 2), DP + TENSOR)
    placed = (
        P(DP, None, TENSOR),
        P(DP, None, TENSOR),
        P(DP, None, TENSOR),
        P(TENSOR, None),
        P(DP, TENSOR, None),
        P(DP, TENSOR),
        P(DP, TENSOR),
        P(DP, TENSOR),
    )
    return jax.shard_map(
        per_device,
        mesh=fine,
        in_specs=placed,
        out_specs=(P(DP, TENSOR), P(DP, TENSOR), P(DP, TENSOR)),
        check_vma=False,
    )
```

```python
import functools

import jax
import jax.numpy as jnp
from jax import lax
from jax.experimental import pallas as pl
from jax.experimental.pallas import tpu as pltpu
from jax.sharding import Mesh, PartitionSpec as P

HEAD = 128
FACTOR = HEAD ** (-0.5)
LOG2E = 1.4426950408889634
BLOCK = 256
SEQ = 1024
DP = ("ylo", "z", "core")
TENSOR = ("x", "yhi")
NT = (((1,), (1,)), ((), ()))
VMEM = pltpu.CompilerParams(vmem_limit_bytes=60 * 1024 * 1024)


def cost(us, moved=0):
    return pl.CostEstimate(flops=int(us * 1.0e9), bytes_accessed=moved, transcendentals=0)


def dot(a, b):
    return jnp.dot(a, b, preferred_element_type=jnp.float32)


def parts_of(number):
    first = number * BLOCK
    own = (first, first + BLOCK)
    return [(0, first), own] if first else [own]


def teacher_kernel(q_ref, k_ref, v_ref, o_ref):
    row = lax.broadcasted_iota(jnp.int32, (BLOCK, BLOCK), 0)
    col = lax.broadcasted_iota(jnp.int32, (BLOCK, BLOCK), 1)
    for number in range(SEQ // BLOCK):
        first = number * BLOCK
        limit = first + BLOCK
        parts = parts_of(number)
        for head in range(2):
            cols = slice(head * HEAD, head * HEAD + HEAD)
            queries = q_ref[first:limit, cols]
            scores = [
                lax.dot_general(queries, k_ref[lo:hi, :], NT, preferred_element_type=jnp.float32)
                for lo, hi in parts
            ]
            scores[-1] = jnp.where(col <= row, scores[-1], -1e30)
            top = functools.reduce(
                jnp.maximum, [jnp.max(s, axis=1, keepdims=True) for s in scores]
            )
            weights = [jnp.exp2((s - top) * (FACTOR * LOG2E)) for s in scores]
            total = sum(jnp.sum(w, axis=1, keepdims=True) for w in weights)
            context = sum(
                dot(w.astype(jnp.bfloat16), v_ref[lo:hi, :]) for w, (lo, hi) in zip(weights, parts)
            )
            o_ref[first:limit, cols] = (context / total).astype(jnp.bfloat16)


def teacher_attention(queries, keys, values, half, before=()):
    steps = queries.shape[1] // (4 * HEAD)
    pair = pl.BlockSpec((SEQ, 2 * HEAD), lambda h: (0, half * steps + h))
    one = pl.BlockSpec((SEQ, HEAD), lambda h: (0, 0))
    return pl.pallas_call(
        lambda q_ref, k_ref, v_ref, *rest: teacher_kernel(q_ref, k_ref, v_ref, rest[-1]),
        grid=(steps,),
        in_specs=[pair, one, one] + [pl.BlockSpec(memory_space=pl.ANY)] * len(before),
        out_specs=pair,
        out_shape=jax.ShapeDtypeStruct(queries.shape, jnp.bfloat16),
        input_output_aliases={3: 0} if before else {},
        compiler_params=VMEM,
        cost_estimate=cost(1 if before else 40),
        name="teacher_attention",
    )(queries, keys, values, *before)


def project_kernel(order_ref, context_ref, p_ref, o_ref):
    o_ref[0] = dot(context_ref[...], p_ref[...]).astype(jnp.bfloat16)


def project(order, context, projector, weight):
    rows = projector.shape[0]
    count = order.shape[0]
    return pl.pallas_call(
        project_kernel,
        grid_spec=pltpu.PrefetchScalarGridSpec(
            num_scalar_prefetch=1,
            grid=(count,),
            in_specs=[
                pl.BlockSpec(context.shape, lambda g, order: (0, 0)),
                pl.BlockSpec((rows, 256), lambda g, order: (0, order[g])),
            ],
            out_specs=pl.BlockSpec((1, SEQ, 256), lambda g, order: (g, 0, 0)),
        ),
        out_shape=jax.ShapeDtypeStruct((count, SEQ, 256), jnp.bfloat16),
        compiler_params=VMEM,
        cost_estimate=cost(weight),
        name="project",
    )(order, context, projector)


def student_project_kernel(count, *refs):
    at_ref, pieces, near_ref, far_ref = refs[0], refs[2 : 2 + count], refs[2 + count], refs[3 + count]
    o_ref, rows_ref, total = refs[-3:]
    step = pl.program_id(0)
    for number, ref in enumerate(pieces):
        rows_ref[pl.ds(pl.multiple_of(at_ref[number], 64), ref.shape[0]), :] = ref[...]

    @pl.when(step == 0)
    def _():
        total[...] = dot(rows_ref[...], near_ref[...])

    @pl.when(step == 1)
    def _():
        total[...] += dot(rows_ref[...], near_ref[...])

    @pl.when(step == 2)
    def _():
        total[...] += dot(rows_ref[...], far_ref[...])

    @pl.when(step == 3)
    def _():
        o_ref[...] = (total[...] + dot(rows_ref[...], far_ref[...])).astype(jnp.bfloat16)


def student_project(places, order, pieces, near, far, before=()):
    depth, cols = near.shape
    half = SEQ // 2
    block = 1024
    side = 1 if before else 0
    count = len(pieces)
    return pl.pallas_call(
        lambda *refs: student_project_kernel(count, *refs),
        grid_spec=pltpu.PrefetchScalarGridSpec(
            num_scalar_prefetch=2,
            grid=(4,),
            in_specs=[
                pl.BlockSpec((p.shape[0], block), lambda k, at, order: (0, order[k]))
                for p in pieces
            ]
            + [
                pl.BlockSpec((block, cols), lambda k, at, order: (jnp.minimum(k, 1), 0)),
                pl.BlockSpec((block, cols), lambda k, at, order: (jnp.maximum(k - 2, 0), 0)),
            ]
            + [pl.BlockSpec(memory_space=pl.ANY)] * len(before),
            out_specs=[
                pl.BlockSpec((half, cols), lambda k, at, order: (side, 0)),
                pl.BlockSpec((half, block), lambda k, at, order: (side, order[k])),
            ],
            scratch_shapes=[pltpu.VMEM((half, cols), jnp.float32)],
        ),
        out_shape=[
            jax.ShapeDtypeStruct((SEQ, cols), jnp.bfloat16),
            jax.ShapeDtypeStruct((SEQ, 2 * depth), jnp.bfloat16),
        ],
        input_output_aliases={4 + count: 0, 5 + count: 1} if before else {},
        compiler_params=VMEM,
        cost_estimate=cost(9),
        name="student_project",
    )(places, order, *pieces, near, far, *before)


def weight_grad_ring_kernel(order_ref, grad_ref, rows_ref, o_ref):
    product = dot(grad_ref[...], rows_ref[...]).astype(jnp.bfloat16)
    o_ref[0, 0, 0] = product[:, :256]
    o_ref[0, 1, 0] = product[:, 256:]


def weight_grad_ring(grads, rows):
    cols = grads.shape[0]
    order = jnp.array([k % 2 * 4 + k // 2 for k in range(8)], jnp.int32)
    return pl.pallas_call(
        weight_grad_ring_kernel,
        grid_spec=pltpu.PrefetchScalarGridSpec(
            num_scalar_prefetch=1,
            grid=(8,),
            in_specs=[
                pl.BlockSpec(grads.shape, lambda k, order: (0, 0)),
                pl.BlockSpec((SEQ, 512), lambda k, order: (0, order[k])),
            ],
            out_specs=pl.BlockSpec(
                (1, 2, 1, cols, 256), lambda k, order: (k // 2, 0, k % 2, 0, 0)
            ),
        ),
        out_shape=jax.ShapeDtypeStruct((4, 2, 2, cols, 256), jnp.bfloat16),
        compiler_params=VMEM,
        cost_estimate=cost(4),
        name="weight_grad_ring",
    )(order, grads, rows)


def weight_grad_kernel(core_ref, order_ref, grad_ref, rows_ref, kept_ref, sent_ref):
    product = dot(grad_ref[...], rows_ref[...]).astype(jnp.bfloat16)

    @pl.when(core_ref[0] == 0)
    def _():
        kept_ref[0] = product[:, :256]
        sent_ref[0] = product[:, 256:]

    @pl.when(core_ref[0] == 1)
    def _():
        kept_ref[0] = product[:, 256:]
        sent_ref[0] = product[:, :256]


def weight_grad(core, order, grads, rows):
    cols = grads.shape[0]
    out = pl.BlockSpec((1, cols, 256), lambda k, core, order: (k, 0, 0))
    return pl.pallas_call(
        weight_grad_kernel,
        grid_spec=pltpu.PrefetchScalarGridSpec(
            num_scalar_prefetch=2,
            grid=(8,),
            in_specs=[
                pl.BlockSpec(grads.shape, lambda k, core, order: (0, 0)),
                pl.BlockSpec((SEQ, 512), lambda k, core, order: (0, order[k])),
            ],
            out_specs=[out, out],
        ),
        out_shape=[jax.ShapeDtypeStruct((8, cols, 256), jnp.bfloat16)] * 2,
        compiler_params=VMEM,
        cost_estimate=cost(4),
        name="weight_grad",
    )(core, order, grads, rows)


def pair_kernel(a_ref, b_ref, *outs):
    for number, ref in enumerate(outs):
        ref[...] = (
            a_ref[number].astype(jnp.float32) + b_ref[number].astype(jnp.float32)
        ).astype(jnp.bfloat16)


def pair_sum(a, b):
    return pl.pallas_call(
        pair_kernel,
        out_shape=[jax.ShapeDtypeStruct(a.shape[1:], jnp.bfloat16) for _ in range(a.shape[0])],
        compiler_params=VMEM,
        cost_estimate=cost(3),
        name="pair_sum",
    )(a, b)


def forward_kernel(y_ref, q_in, k_in, v_in, q_ref, kv_ref, probs_ref, context_ref, vt):
    y = y_ref[0]
    for block in range(4):
        for which, side in ((0, y), (1, 1 - y)):
            rows = slice((4 * which + block) * HEAD, (4 * which + block) * HEAD + HEAD)
            at = pl.ds(pl.multiple_of((2 * block + side) * HEAD, HEAD), HEAD)
            q_ref[at, :] = q_in[rows, :]
            kv_ref[at, :HEAD] = k_in[rows, :]
            kv_ref[at, HEAD:] = v_in[rows, :]
    vt[...] = kv_ref[:, HEAD:].T
    key = lax.broadcasted_iota(jnp.int32, (BLOCK, BLOCK), 0)
    query = lax.broadcasted_iota(jnp.int32, (BLOCK, BLOCK), 1)
    for number in range(SEQ // BLOCK):
        first = number * BLOCK
        limit = first + BLOCK
        parts = parts_of(number)
        for head in range(2):
            cols = slice(head * HEAD, head * HEAD + HEAD)
            queries = q_ref[first:limit, cols]
            scores = [
                lax.dot_general(
                    kv_ref[lo:hi, :HEAD], queries, NT, preferred_element_type=jnp.float32
                )
                for lo, hi in parts
            ]
            scores[-1] = jnp.where(key <= query, scores[-1], -1e30)
            top = functools.reduce(
                jnp.maximum, [jnp.max(s, axis=0, keepdims=True) for s in scores]
            )
            weights = [jnp.exp2((s - top) * (FACTOR * LOG2E)) for s in scores]
            scale = 1.0 / sum(jnp.sum(w, axis=0, keepdims=True) for w in weights)
            context = 0.0
            for w, (lo, hi) in zip(weights, parts):
                rounded = (w * scale).astype(jnp.bfloat16)
                probs_ref[head, lo:hi, first:limit] = rounded
                context += dot(vt[:, lo:hi], rounded)
            context_ref[first:limit, cols] = context.T


def student_forward(y, projected):
    pair = pl.BlockSpec((SEQ, 2 * HEAD), lambda i, y: (0, i))
    both = pl.BlockSpec((SEQ, 2 * HEAD), lambda i, y: (0, 0))
    return pl.pallas_call(
        forward_kernel,
        grid_spec=pltpu.PrefetchScalarGridSpec(
            num_scalar_prefetch=1,
            grid=(2,),
            in_specs=[
                pair,
                pl.BlockSpec((SEQ, HEAD), lambda i, y: (0, 4)),
                pl.BlockSpec((SEQ, HEAD), lambda i, y: (0, 5)),
            ],
            out_specs=[pair, both, pl.BlockSpec((2, SEQ, SEQ), lambda i, y: (i, 0, 0)), pair],
            scratch_shapes=[pltpu.VMEM((HEAD, SEQ), jnp.bfloat16)],
        ),
        out_shape=[
            jax.ShapeDtypeStruct((SEQ, 4 * HEAD), jnp.bfloat16),
            jax.ShapeDtypeStruct((SEQ, 2 * HEAD), jnp.bfloat16),
            jax.ShapeDtypeStruct((4, SEQ, SEQ), jnp.bfloat16),
            jax.ShapeDtypeStruct((SEQ, 4 * HEAD), jnp.float32),
        ],
        compiler_params=VMEM,
        cost_estimate=cost(12),
        name="student_forward",
    )(y, projected, projected, projected)


def backward_kernel(has_start, y_ref, q_ref, kv_ref, probs_ref, context_ref, mine_ref, *rest):
    if has_start:
        start_ref, grad_ref, kt, dk, dv = rest
        dk[...] = start_ref[:, :HEAD]
        dv[...] = start_ref[:, HEAD:]
    else:
        theirs_ref, grad_ref, gkv_ref, kt, dk, dv = rest
        dk[...] = jnp.zeros_like(dk)
        dv[...] = jnp.zeros_like(dv)
    y = y_ref[0]
    kt[...] = kv_ref[:, :HEAD].T

    def store(at, block, value):
        for which, side in ((0, y), (1, 1 - y)):
            lanes = pl.ds(pl.multiple_of((4 * side + block) * HEAD, HEAD), HEAD)
            grad_ref[at, lanes] = value[:, which * HEAD : which * HEAD + HEAD]

    for number in range(SEQ // BLOCK):
        first = number * BLOCK
        limit = first + BLOCK
        parts = parts_of(number)
        for head in range(2):
            cols = slice(head * HEAD, head * HEAD + HEAD)
            queries = q_ref[first:limit, cols]
            target = mine_ref[0, first:limit, cols].astype(jnp.float32)
            if not has_start:
                target += theirs_ref[first:limit, cols].astype(jnp.float32)
            incoming = ((context_ref[first:limit, cols] - target) * (1.0 / 16)).astype(
                jnp.bfloat16
            )
            rounded = [probs_ref[head, lo:hi, first:limit] for lo, hi in parts]
            probs = [r.astype(jnp.float32) for r in rounded]
            grad_probs = [
                lax.dot_general(
                    kv_ref[lo:hi, HEAD:], incoming, NT, preferred_element_type=jnp.float32
                )
                for lo, hi in parts
            ]
            inner = sum(
                jnp.sum(g * p, axis=0, keepdims=True) for g, p in zip(grad_probs, probs)
            )
            scaled = [
                (p * (g - inner)).astype(jnp.bfloat16) for g, p in zip(grad_probs, probs)
            ]
            for r, s, (lo, hi) in zip(rounded, scaled, parts):
                dv[lo:hi, :] += dot(r, incoming)
                dk[lo:hi, :] += dot(s, queries)
            grad = sum(dot(kt[:, lo:hi], s) for s, (lo, hi) in zip(scaled, parts))
            store(cols, number, (grad * FACTOR).astype(jnp.bfloat16))

    if has_start:
        for number in range(SEQ // BLOCK):
            rows = slice(number * BLOCK, number * BLOCK + BLOCK)
            store(slice(256, 384), number, (dk[rows, :] * FACTOR).T.astype(jnp.bfloat16))
            store(slice(384, 512), number, dv[rows, :].T.astype(jnp.bfloat16))
    else:
        gkv_ref[:, :HEAD] = dk[...]
        gkv_ref[:, HEAD:] = dv[...]


def student_backward(y, forward, mine, part, theirs=None, start=None):
    queries, kv, probs, context = forward
    pair = pl.BlockSpec((SEQ, 2 * HEAD), lambda i, y: (0, part))
    whole = pl.BlockSpec((SEQ, 2 * HEAD), lambda i, y: (0, 0))
    columns = 256 if start is None else 512
    grad = pl.BlockSpec((columns, SEQ), lambda i, y: (0, 0))
    grad_shape = jax.ShapeDtypeStruct((columns, SEQ), jnp.bfloat16)
    target = (lambda i, y: (y[0], 0, 0)) if start is None else (lambda i, y: (0, 0, 0))
    return pl.pallas_call(
        lambda *refs: backward_kernel(start is not None, *refs),
        grid_spec=pltpu.PrefetchScalarGridSpec(
            num_scalar_prefetch=1,
            grid=(1,),
            in_specs=[
                pair,
                whole,
                pl.BlockSpec((2, SEQ, SEQ), lambda i, y: (part, 0, 0)),
                pair,
                pl.BlockSpec((1, SEQ, 2 * HEAD), target),
                whole,
            ],
            out_specs=[grad, whole] if start is None else [grad],
            scratch_shapes=[
                pltpu.VMEM((HEAD, SEQ), jnp.bfloat16),
                pltpu.VMEM((SEQ, HEAD), jnp.float32),
                pltpu.VMEM((SEQ, HEAD), jnp.float32),
            ],
        ),
        out_shape=[grad_shape, jax.ShapeDtypeStruct((SEQ, 2 * HEAD), jnp.float32)]
        if start is None
        else [grad_shape],
        compiler_params=VMEM,
        cost_estimate=cost(8),
        name="student_backward",
    )(y, queries, kv, probs, context, mine, theirs if start is None else start)


def shift(array, axis, step=1):
    n = lax.axis_size(axis)
    return lax.ppermute(array, axis, [(i, (i + step) % n) for i in range(n)])


def gather_rows_near(own):
    return shift(own, "yhi"), shift(own, "x", 1), shift(own, "x", -1)


def far_halves(left, right):
    half = left.shape[0] // 2
    return shift(left[:half], "x", 1), shift(right[half:], "x", -1)


def row_places(x):
    places = [(x + dx) % 4 * 128 + offset for dx, offset in ((0, 0), (3, 0), (1, 0), (2, 0), (2, 64))]
    return jnp.stack(places).astype(jnp.int32)


RELATIVE = [(dy, dz) for dy in range(2) for dz in range(4)]


def row_blocks():
    y = lax.axis_index("ylo")
    z = lax.axis_index("z")
    return jnp.stack([(y + dy) % 2 * 4 + (z + dz) % 4 for dy, dz in RELATIVE]).astype(jnp.int32)


def send_direct(blocks):
    got = [blocks[0]]
    for (dy, dz), block in zip(RELATIVE[1:], blocks[1:]):
        route = [(i * 4 + k, (i + dy) % 2 * 4 + (k + dz) % 4) for i in range(2) for k in range(4)]
        got.append(lax.ppermute(block, ("ylo", "z"), route))
    return got


def finish_kernel(*refs):
    a_refs, b_refs, (q_ref, k_ref, v_ref) = refs[:2], refs[2:10], refs[10:]

    def total(parts):
        result = parts[0][...].astype(jnp.float32)
        for part in parts[1:]:
            result += part[...].astype(jnp.float32)
        return result.T

    q_ref[:, :256] = total(a_refs)
    rest = total(b_refs)
    q_ref[:, 256:] = rest[:, :256]
    k_ref[...] = rest[:, 256:384]
    v_ref[...] = rest[:, 384:]


def finish(got_a, got_b):
    return pl.pallas_call(
        finish_kernel,
        out_shape=[jax.ShapeDtypeStruct((256, cols), jnp.float32) for cols in (512, 128, 128)],
        compiler_params=VMEM,
        cost_estimate=cost(3),
        name="finish",
    )(*got_a, *got_b)


def per_device(
    teacher_queries,
    teacher_keys,
    teacher_values,
    projector,
    student_inputs,
    query_weight,
    key_weight,
    value_weight,
):
    tq, tk, tv = teacher_queries[0], teacher_keys[0], teacher_values[0]
    x, yhi, ylo = lax.axis_index("x"), lax.axis_index("yhi"), lax.axis_index("ylo")
    own = student_inputs[0]
    other, left, right = gather_rows_near(own)
    shard = jnp.concatenate([query_weight, key_weight, value_weight], axis=1)

    groups = jnp.arange(4, dtype=jnp.int32)
    context = teacher_attention(tq, tk, tv, 0)
    near = lax.all_gather(shard, ("z", "core"), axis=0, tiled=True)
    shard_far = shift(shard, "ylo")
    context, left, right, other, shard_far = lax.optimization_barrier(
        (context, left, right, other, shard_far)
    )
    context = teacher_attention(tq, tk, tv, 1, (context,))
    sent = project(2 * (2 * groups + 1 - yhi) + 1, context, projector, 1)
    far = lax.all_gather(shard_far, ("z", "core"), axis=0, tiled=True)
    came = shift(sent, "yhi")
    product_a = project(2 * jnp.arange(8, dtype=jnp.int32), context, projector, 1)
    sum_a = lax.psum_scatter(product_a, "x", scatter_dimension=0, tiled=True)

    own_far = far_halves(left, right)
    other_left, other_right = shift(other, "x", 1), shift(other, "x", -1)
    context, other_left, other_right, own_far, near, far = lax.optimization_barrier(
        (context, other_left, other_right, own_far, near, far)
    )
    kept = project(2 * (2 * groups + yhi) + 1, context, projector, 150)
    other_far = far_halves(other_left, other_right)

    places = row_places(x)
    order = jnp.stack([2 * ylo, 2 * ylo + 1, 2 - 2 * ylo, 3 - 2 * ylo]).astype(jnp.int32)
    before = student_project(places, order, [own, left, right, *own_far], near, far)
    came, before, *other_far = lax.optimization_barrier((came, before, *other_far))
    both = (kept.astype(jnp.float32) + came.astype(jnp.float32)).astype(jnp.bfloat16)
    sum_b = lax.psum_scatter(both, "x", scatter_dimension=0, tiled=True)
    projected, rows = student_project(
        places, order, [other, other_left, other_right, *other_far], near, far, before
    )

    y = yhi.astype(jnp.int32).reshape(1)
    theirs_a = shift(lax.dynamic_index_in_dim(sum_a, 1 - yhi, 0, keepdims=False), "yhi")
    core = lax.axis_index("core").astype(jnp.int32).reshape(1)
    forward = student_forward(y, projected)
    forward, theirs_a = lax.optimization_barrier((forward, theirs_a))

    grad_a, part_kv = student_backward(y, forward, sum_a, 0, theirs=theirs_a)
    whole_a = weight_grad_ring(grad_a, rows)
    ring_a = lax.psum_scatter(
        whole_a.reshape(16, 256, 256), ("z", "core"), scatter_dimension=0, tiled=True
    )
    sum_b, whole_a = lax.optimization_barrier((sum_b, whole_a))
    (grad_b,) = student_backward(y, forward, sum_b, 1, start=part_kv)
    kept_b, sent_b = weight_grad(core, row_blocks(), grad_b, rows)
    got_b = send_direct(list(pair_sum(kept_b, shift(sent_b, "core"))))
    theirs = shift(lax.dynamic_index_in_dim(ring_a, 1 - ylo, 0, keepdims=False), "ylo")
    mine = lax.dynamic_index_in_dim(ring_a, ylo, 0, keepdims=False)
    return tuple(finish([mine, theirs], got_b))


def solution(mesh):
    fine = Mesh(mesh.devices.reshape(2, 4, 2, 4, 2), DP + TENSOR)
    placed = (
        P(DP, None, TENSOR),
        P(DP, None, TENSOR),
        P(DP, None, TENSOR),
        P(TENSOR, None),
        P(DP, TENSOR, None),
        P(DP, TENSOR),
        P(DP, TENSOR),
        P(DP, TENSOR),
    )
    return jax.shard_map(
        per_device,
        mesh=fine,
        in_specs=placed,
        out_specs=(P(DP, TENSOR), P(DP, TENSOR), P(DP, TENSOR)),
        check_vma=False,
    )
```

```python
import functools

import jax
import jax.numpy as jnp
from jax import lax
from jax.experimental import pallas as pl
from jax.experimental.pallas import tpu as pltpu
from jax.sharding import Mesh, PartitionSpec as P

HEAD = 128
FACTOR = HEAD ** (-0.5)
LOG2E = 1.4426950408889634
BLOCK = 256
SEQ = 1024
DP = ("ylo", "z", "core")
TENSOR = ("x", "yhi")
NT = (((1,), (1,)), ((), ()))
VMEM = pltpu.CompilerParams(vmem_limit_bytes=60 * 1024 * 1024)


def cost(us, moved=0):
    return pl.CostEstimate(flops=int(us * 1.0e9), bytes_accessed=moved, transcendentals=0)


def dot(a, b):
    return jnp.dot(a, b, preferred_element_type=jnp.float32)


def parts_of(number):
    first = number * BLOCK
    own = (first, first + BLOCK)
    return [(0, first), own] if first else [own]


def teacher_kernel(q_ref, k_ref, v_ref, o_ref):
    row = lax.broadcasted_iota(jnp.int32, (BLOCK, BLOCK), 0)
    col = lax.broadcasted_iota(jnp.int32, (BLOCK, BLOCK), 1)
    for number in range(SEQ // BLOCK):
        first = number * BLOCK
        limit = first + BLOCK
        parts = parts_of(number)
        for head in range(2):
            cols = slice(head * HEAD, head * HEAD + HEAD)
            queries = q_ref[first:limit, cols]
            scores = [
                lax.dot_general(queries, k_ref[lo:hi, :], NT, preferred_element_type=jnp.float32)
                for lo, hi in parts
            ]
            scores[-1] = jnp.where(col <= row, scores[-1], -1e30)
            top = functools.reduce(
                jnp.maximum, [jnp.max(s, axis=1, keepdims=True) for s in scores]
            )
            weights = [jnp.exp2((s - top) * (FACTOR * LOG2E)) for s in scores]
            total = sum(jnp.sum(w, axis=1, keepdims=True) for w in weights)
            context = sum(
                dot(w.astype(jnp.bfloat16), v_ref[lo:hi, :]) for w, (lo, hi) in zip(weights, parts)
            )
            o_ref[first:limit, cols] = (context / total).astype(jnp.bfloat16)


def teacher_attention(queries, keys, values, half, before=()):
    steps = queries.shape[1] // (4 * HEAD)
    pair = pl.BlockSpec((SEQ, 2 * HEAD), lambda h: (0, half * steps + h))
    one = pl.BlockSpec((SEQ, HEAD), lambda h: (0, 0))
    return pl.pallas_call(
        lambda q_ref, k_ref, v_ref, *rest: teacher_kernel(q_ref, k_ref, v_ref, rest[-1]),
        grid=(steps,),
        in_specs=[pair, one, one] + [pl.BlockSpec(memory_space=pl.ANY)] * len(before),
        out_specs=pair,
        out_shape=jax.ShapeDtypeStruct(queries.shape, jnp.bfloat16),
        input_output_aliases={3: 0} if before else {},
        compiler_params=VMEM,
        cost_estimate=cost(150 if before else 40),
        name="teacher_attention",
    )(queries, keys, values, *before)


def project_kernel(order_ref, context_ref, a_ref, b_ref, o_ref):
    o_ref[0] = dot(context_ref[...], a_ref[...]).astype(jnp.bfloat16)
    o_ref[1] = dot(context_ref[...], b_ref[...]).astype(jnp.bfloat16)


def project(order, context, projector, weight):
    rows = projector.shape[0]
    count = order.shape[0]
    return pl.pallas_call(
        project_kernel,
        grid_spec=pltpu.PrefetchScalarGridSpec(
            num_scalar_prefetch=1,
            grid=(count // 2,),
            in_specs=[
                pl.BlockSpec(context.shape, lambda g, order: (0, 0)),
                pl.BlockSpec((rows, 256), lambda g, order: (0, order[2 * g])),
                pl.BlockSpec((rows, 256), lambda g, order: (0, order[2 * g + 1])),
            ],
            out_specs=pl.BlockSpec((2, SEQ, 256), lambda g, order: (g, 0, 0)),
        ),
        out_shape=jax.ShapeDtypeStruct((count, SEQ, 256), jnp.bfloat16),
        compiler_params=VMEM,
        cost_estimate=cost(weight),
        name="project",
    )(order, context, projector, projector)


def student_project_kernel(count, *refs):
    at_ref, pieces, near_ref, far_ref = refs[0], refs[2 : 2 + count], refs[2 + count], refs[3 + count]
    o_ref, rows_ref, total = refs[-3:]
    step = pl.program_id(0)
    for number, ref in enumerate(pieces):
        rows_ref[pl.ds(pl.multiple_of(at_ref[number], 64), ref.shape[0]), :] = ref[...]

    @pl.when(step == 0)
    def _():
        total[...] = dot(rows_ref[...], near_ref[...])

    @pl.when(step == 1)
    def _():
        o_ref[...] = (total[...] + dot(rows_ref[...], far_ref[...])).astype(jnp.bfloat16)


def student_project(places, order, pieces, near, far, before=()):
    depth, cols = near.shape
    half = SEQ // 2
    block = depth
    side = 1 if before else 0
    count = len(pieces)
    return pl.pallas_call(
        lambda *refs: student_project_kernel(count, *refs),
        grid_spec=pltpu.PrefetchScalarGridSpec(
            num_scalar_prefetch=2,
            grid=(2,),
            in_specs=[
                pl.BlockSpec((p.shape[0], block), lambda k, at, order: (0, order[k]))
                for p in pieces
            ]
            + [
                pl.BlockSpec((block, cols), lambda k, at, order: (0, 0)),
                pl.BlockSpec((block, cols), lambda k, at, order: (0, 0)),
            ]
            + [pl.BlockSpec(memory_space=pl.ANY)] * len(before),
            out_specs=[
                pl.BlockSpec((half, cols), lambda k, at, order: (side, 0)),
                pl.BlockSpec((half, block), lambda k, at, order: (side, order[k])),
            ],
            scratch_shapes=[pltpu.VMEM((half, cols), jnp.float32)],
        ),
        out_shape=[
            jax.ShapeDtypeStruct((SEQ, cols), jnp.bfloat16),
            jax.ShapeDtypeStruct((SEQ, 2 * depth), jnp.bfloat16),
        ],
        input_output_aliases={4 + count: 0, 5 + count: 1} if before else {},
        compiler_params=VMEM,
        cost_estimate=cost(9 if before else 0),
        name="student_project",
    )(places, order, *pieces, near, far, *before)


def weight_grad_ring_kernel(grad_ref, rows_ref, o_ref):
    product = dot(grad_ref[...], rows_ref[...]).astype(jnp.bfloat16)
    for z in range(2):
        for core in range(2):
            at = (2 * z + core) * 256
            o_ref[z, core, 0] = product[:, at : at + 256]


def weight_grad_ring(grads, rows):
    cols = grads.shape[0]
    return pl.pallas_call(
        weight_grad_ring_kernel,
        grid=(4,),
        in_specs=[
            pl.BlockSpec(grads.shape, lambda k: (0, 0)),
            pl.BlockSpec((SEQ, 1024), lambda k: (0, k)),
        ],
        out_specs=pl.BlockSpec((2, 2, 1, cols, 256), lambda k: (k % 2, 0, k // 2, 0, 0)),
        out_shape=jax.ShapeDtypeStruct((4, 2, 2, cols, 256), jnp.bfloat16),
        compiler_params=VMEM,
        cost_estimate=cost(4),
        name="weight_grad_ring",
    )(grads, rows)


def weight_grad_kernel(core_ref, grad_ref, rows_ref, kept_ref, sent_ref):
    product = dot(grad_ref[...], rows_ref[...]).astype(jnp.bfloat16)

    def store(first, second):
        for z in range(2):
            first[z] = product[:, 512 * z : 512 * z + 256]
            second[z] = product[:, 512 * z + 256 : 512 * z + 512]

    @pl.when(core_ref[0] == 0)
    def _():
        store(kept_ref, sent_ref)

    @pl.when(core_ref[0] == 1)
    def _():
        store(sent_ref, kept_ref)


def weight_grad(core, grads, rows):
    cols = grads.shape[0]
    out = pl.BlockSpec((2, cols, 256), lambda k, core: (k, 0, 0))
    return pl.pallas_call(
        weight_grad_kernel,
        grid_spec=pltpu.PrefetchScalarGridSpec(
            num_scalar_prefetch=1,
            grid=(4,),
            in_specs=[
                pl.BlockSpec(grads.shape, lambda k, core: (0, 0)),
                pl.BlockSpec((SEQ, 1024), lambda k, core: (0, k)),
            ],
            out_specs=[out, out],
        ),
        out_shape=[jax.ShapeDtypeStruct((8, cols, 256), jnp.bfloat16)] * 2,
        compiler_params=VMEM,
        cost_estimate=cost(4),
        name="weight_grad",
    )(core, grads, rows)


def pair_kernel(order_ref, a_ref, b_ref, *outs):
    for number, ref in enumerate(outs):
        at = order_ref[number]
        ref[...] = (a_ref[at].astype(jnp.float32) + b_ref[at].astype(jnp.float32)).astype(
            jnp.bfloat16
        )


def pair_sum(order, a, b):
    whole = pl.BlockSpec(a.shape, lambda i, order: (0, 0, 0))
    one = pl.BlockSpec(a.shape[1:], lambda i, order: (0, 0))
    return pl.pallas_call(
        pair_kernel,
        grid_spec=pltpu.PrefetchScalarGridSpec(
            num_scalar_prefetch=1,
            grid=(1,),
            in_specs=[whole, whole],
            out_specs=[one] * a.shape[0],
        ),
        out_shape=[jax.ShapeDtypeStruct(a.shape[1:], jnp.bfloat16) for _ in range(a.shape[0])],
        compiler_params=VMEM,
        cost_estimate=cost(3),
        name="pair_sum",
    )(order, a, b)


def forward_kernel(y_ref, q_in, k_in, v_in, q_ref, kv_ref, probs_ref, context_ref, vt):
    y = y_ref[0]
    for block in range(4):
        for which, side in ((0, y), (1, 1 - y)):
            rows = slice((4 * which + block) * HEAD, (4 * which + block) * HEAD + HEAD)
            at = pl.ds(pl.multiple_of((2 * block + side) * HEAD, HEAD), HEAD)
            q_ref[at, :] = q_in[rows, :]
            kv_ref[at, :HEAD] = k_in[rows, :]
            kv_ref[at, HEAD:] = v_in[rows, :]
    vt[...] = kv_ref[:, HEAD:].T
    key = lax.broadcasted_iota(jnp.int32, (BLOCK, BLOCK), 0)
    query = lax.broadcasted_iota(jnp.int32, (BLOCK, BLOCK), 1)
    for number in range(SEQ // BLOCK):
        first = number * BLOCK
        limit = first + BLOCK
        parts = parts_of(number)
        for head in range(2):
            cols = slice(head * HEAD, head * HEAD + HEAD)
            queries = q_ref[first:limit, cols]
            scores = [
                lax.dot_general(
                    kv_ref[lo:hi, :HEAD], queries, NT, preferred_element_type=jnp.float32
                )
                for lo, hi in parts
            ]
            scores[-1] = jnp.where(key <= query, scores[-1], -1e30)
            top = functools.reduce(
                jnp.maximum, [jnp.max(s, axis=0, keepdims=True) for s in scores]
            )
            weights = [jnp.exp2((s - top) * (FACTOR * LOG2E)) for s in scores]
            scale = 1.0 / sum(jnp.sum(w, axis=0, keepdims=True) for w in weights)
            context = 0.0
            for w, (lo, hi) in zip(weights, parts):
                rounded = (w * scale).astype(jnp.bfloat16)
                probs_ref[head, lo:hi, first:limit] = rounded
                context += dot(vt[:, lo:hi], rounded)
            context_ref[first:limit, cols] = context.T


def student_forward(y, projected):
    pair = pl.BlockSpec((SEQ, 2 * HEAD), lambda i, y: (0, i))
    both = pl.BlockSpec((SEQ, 2 * HEAD), lambda i, y: (0, 0))
    return pl.pallas_call(
        forward_kernel,
        grid_spec=pltpu.PrefetchScalarGridSpec(
            num_scalar_prefetch=1,
            grid=(2,),
            in_specs=[
                pair,
                pl.BlockSpec((SEQ, HEAD), lambda i, y: (0, 4)),
                pl.BlockSpec((SEQ, HEAD), lambda i, y: (0, 5)),
            ],
            out_specs=[pair, both, pl.BlockSpec((2, SEQ, SEQ), lambda i, y: (i, 0, 0)), pair],
            scratch_shapes=[pltpu.VMEM((HEAD, SEQ), jnp.bfloat16)],
        ),
        out_shape=[
            jax.ShapeDtypeStruct((SEQ, 4 * HEAD), jnp.bfloat16),
            jax.ShapeDtypeStruct((SEQ, 2 * HEAD), jnp.bfloat16),
            jax.ShapeDtypeStruct((4, SEQ, SEQ), jnp.bfloat16),
            jax.ShapeDtypeStruct((SEQ, 4 * HEAD), jnp.float32),
        ],
        compiler_params=VMEM,
        cost_estimate=cost(60),
        name="student_forward",
    )(y, projected, projected, projected)


def backward_kernel(count, has_start, y_ref, q_ref, kv_ref, probs_ref, context_ref, *rest):
    targets, rest = rest[:count], rest[count:]
    if has_start:
        start_ref, grad_ref, kt, dk, dv = rest
        dk[...] = start_ref[:, :HEAD]
        dv[...] = start_ref[:, HEAD:]
    else:
        grad_ref, gkv_ref, kt, dk, dv = rest
        dk[...] = jnp.zeros_like(dk)
        dv[...] = jnp.zeros_like(dv)
    y = y_ref[0]
    kt[...] = kv_ref[:, :HEAD].T

    def store(at, block, value):
        for which, side in ((0, y), (1, 1 - y)):
            lanes = pl.ds(pl.multiple_of((4 * side + block) * HEAD, HEAD), HEAD)
            grad_ref[at, lanes] = value[:, which * HEAD : which * HEAD + HEAD]

    for number in range(SEQ // BLOCK):
        first = number * BLOCK
        limit = first + BLOCK
        parts = parts_of(number)
        for head in range(2):
            cols = slice(head * HEAD, head * HEAD + HEAD)
            queries = q_ref[first:limit, cols]
            target = 0.0
            for part in targets:
                target += part[0, first:limit, cols].astype(jnp.float32)
            incoming = ((context_ref[first:limit, cols] - target) * (1.0 / 16)).astype(
                jnp.bfloat16
            )
            rounded = [probs_ref[head, lo:hi, first:limit] for lo, hi in parts]
            probs = [r.astype(jnp.float32) for r in rounded]
            grad_probs = [
                lax.dot_general(
                    kv_ref[lo:hi, HEAD:], incoming, NT, preferred_element_type=jnp.float32
                )
                for lo, hi in parts
            ]
            inner = sum(
                jnp.sum(g * p, axis=0, keepdims=True) for g, p in zip(grad_probs, probs)
            )
            scaled = [
                (p * (g - inner)).astype(jnp.bfloat16) for g, p in zip(grad_probs, probs)
            ]
            for r, s, (lo, hi) in zip(rounded, scaled, parts):
                dv[lo:hi, :] += dot(r, incoming)
                dk[lo:hi, :] += dot(s, queries)
            grad = sum(dot(kt[:, lo:hi], s) for s, (lo, hi) in zip(scaled, parts))
            store(cols, number, (grad * FACTOR).astype(jnp.bfloat16))

    if has_start:
        for number in range(SEQ // BLOCK):
            rows = slice(number * BLOCK, number * BLOCK + BLOCK)
            store(slice(256, 384), number, (dk[rows, :] * FACTOR).T.astype(jnp.bfloat16))
            store(slice(384, 512), number, dv[rows, :].T.astype(jnp.bfloat16))
    else:
        gkv_ref[:, :HEAD] = dk[...]
        gkv_ref[:, HEAD:] = dv[...]


def student_backward(y, forward, targets, part, start=None):
    queries, kv, probs, context = forward
    pair = pl.BlockSpec((SEQ, 2 * HEAD), lambda i, y: (0, part))
    whole = pl.BlockSpec((SEQ, 2 * HEAD), lambda i, y: (0, 0))
    columns = 256 if start is None else 512
    grad = pl.BlockSpec((columns, SEQ), lambda i, y: (0, 0))
    grad_shape = jax.ShapeDtypeStruct((columns, SEQ), jnp.bfloat16)
    at_side = pl.BlockSpec((1, SEQ, 2 * HEAD), lambda i, y: (y[0], 0, 0))
    alone = pl.BlockSpec((1, SEQ, 2 * HEAD), lambda i, y: (0, 0, 0))
    return pl.pallas_call(
        lambda *refs: backward_kernel(len(targets), start is not None, *refs),
        grid_spec=pltpu.PrefetchScalarGridSpec(
            num_scalar_prefetch=1,
            grid=(1,),
            in_specs=[pair, whole, pl.BlockSpec((2, SEQ, SEQ), lambda i, y: (part, 0, 0)), pair]
            + [alone if t.shape[0] == 1 else at_side for t in targets]
            + [whole] * (start is not None),
            out_specs=[grad, whole] if start is None else [grad],
            scratch_shapes=[
                pltpu.VMEM((HEAD, SEQ), jnp.bfloat16),
                pltpu.VMEM((SEQ, HEAD), jnp.float32),
                pltpu.VMEM((SEQ, HEAD), jnp.float32),
            ],
        ),
        out_shape=[grad_shape, jax.ShapeDtypeStruct((SEQ, 2 * HEAD), jnp.float32)]
        if start is None
        else [grad_shape],
        compiler_params=VMEM,
        cost_estimate=cost(8),
        name="student_backward",
    )(y, queries, kv, probs, context, *targets, *([] if start is None else [start]))


def shift(array, axis, step=1):
    n = lax.axis_size(axis)
    return lax.ppermute(array, axis, [(i, (i + step) % n) for i in range(n)])


def gather_rows_near(own):
    return shift(own, "yhi"), shift(own, "x", 1), shift(own, "x", -1)


def far_halves(left, right):
    half = left.shape[0] // 2
    return shift(left[:half], "x", 1), shift(right[half:], "x", -1)


def row_places(x):
    places = [(x + dx) % 4 * 128 + offset for dx, offset in ((0, 0), (3, 0), (1, 0), (2, 0), (2, 64))]
    return jnp.stack(places).astype(jnp.int32)


RELATIVE = [(dy, dz) for dy in range(2) for dz in range(4)]


def row_blocks():
    y = lax.axis_index("ylo")
    z = lax.axis_index("z")
    return jnp.stack([(y + dy) % 2 * 4 + (z + dz) % 4 for dy, dz in RELATIVE]).astype(jnp.int32)


def send_direct(blocks):
    got = [blocks[0]]
    for (dy, dz), block in zip(RELATIVE[1:], blocks[1:]):
        route = [(i * 4 + k, (i + dy) % 2 * 4 + (k + dz) % 4) for i in range(2) for k in range(4)]
        got.append(lax.ppermute(block, ("ylo", "z"), route))
    return got


def finish_kernel(*refs):
    a_refs, b_refs, (q_ref, k_ref, v_ref) = refs[:2], refs[2:10], refs[10:]

    def total(parts):
        result = parts[0][...].astype(jnp.float32)
        for part in parts[1:]:
            result += part[...].astype(jnp.float32)
        return result.T

    q_ref[:, :256] = total(a_refs)
    rest = total(b_refs)
    q_ref[:, 256:] = rest[:, :256]
    k_ref[...] = rest[:, 256:384]
    v_ref[...] = rest[:, 384:]


def finish(got_a, got_b):
    return pl.pallas_call(
        finish_kernel,
        out_shape=[jax.ShapeDtypeStruct((256, cols), jnp.float32) for cols in (512, 128, 128)],
        compiler_params=VMEM,
        cost_estimate=cost(3),
        name="finish",
    )(*got_a, *got_b)


def per_device(
    teacher_queries,
    teacher_keys,
    teacher_values,
    projector,
    student_inputs,
    query_weight,
    key_weight,
    value_weight,
):
    tq, tk, tv = teacher_queries[0], teacher_keys[0], teacher_values[0]
    x, yhi, ylo = lax.axis_index("x"), lax.axis_index("yhi"), lax.axis_index("ylo")
    own = student_inputs[0]
    other, left, right = gather_rows_near(own)

    groups = jnp.arange(4, dtype=jnp.int32)
    context = teacher_attention(tq, tk, tv, 0)
    context, query_weight, key_weight, value_weight = lax.optimization_barrier(
        (context, query_weight, key_weight, value_weight)
    )
    shard = jnp.concatenate([query_weight, key_weight, value_weight], axis=1)
    near = lax.all_gather(shard, ("z", "core"), axis=0, tiled=True)
    shard_far = shift(shard, "ylo")
    context = teacher_attention(tq, tk, tv, 1, (context,))
    context, left, right, other, shard_far = lax.optimization_barrier(
        (context, left, right, other, shard_far)
    )
    far = lax.all_gather(shard_far, ("z", "core"), axis=0, tiled=True)
    sent = project(2 * (2 * groups + 1 - yhi), context, projector, 0)
    came = shift(sent, "yhi")

    product_b = project(2 * jnp.arange(8, dtype=jnp.int32) + 1, context, projector, 0)

    own_far = far_halves(left, right)
    other_left, other_right = shift(other, "x", 1), shift(other, "x", -1)
    sum_b = lax.psum_scatter(product_b, "x", scatter_dimension=0, tiled=True)
    context, other_left, other_right, own_far, product_b = lax.optimization_barrier(
        (context, other_left, other_right, own_far, product_b)
    )
    kept = project(2 * (2 * groups + yhi), context, projector, 30)
    other_far = far_halves(other_left, other_right)

    places = row_places(x)
    order = jnp.stack([ylo, 1 - ylo]).astype(jnp.int32)
    before = student_project(places, order, [own, left, right, *own_far], near, far)
    came, before, *other_far = lax.optimization_barrier((came, before, *other_far))
    by_x = ((x + jnp.arange(4)) % 4).astype(jnp.int32)
    blocks_a = pair_sum(by_x, kept, came)
    targets_a = [blocks_a[0][None]] + [
        shift(block, "x", step)[None] for step, block in enumerate(blocks_a) if step
    ]
    projected, rows = student_project(
        places, order, [other, other_left, other_right, *other_far], near, far, before
    )

    y = yhi.astype(jnp.int32).reshape(1)
    core = lax.axis_index("core").astype(jnp.int32).reshape(1)
    forward = student_forward(y, projected)
    forward, targets_a = lax.optimization_barrier((forward, targets_a))

    grad_a, part_kv = student_backward(y, forward, targets_a, 0)
    sum_b, grad_a = lax.optimization_barrier((sum_b, grad_a))
    theirs_b = shift(lax.dynamic_slice_in_dim(sum_b, 1 - yhi, 1, 0), "yhi")
    whole_a = weight_grad_ring(grad_a, rows)
    ring_a = lax.psum_scatter(
        whole_a.reshape(16, 256, 256), ("z", "core"), scatter_dimension=0, tiled=True
    )
    theirs_b, whole_a = lax.optimization_barrier((theirs_b, whole_a))
    (grad_b,) = student_backward(y, forward, [sum_b, theirs_b], 1, start=part_kv)
    kept_b, sent_b = weight_grad(core, grad_b, rows)
    got_b = send_direct(list(pair_sum(row_blocks(), kept_b, shift(sent_b, "core"))))
    theirs = shift(lax.dynamic_index_in_dim(ring_a, 1 - ylo, 0, keepdims=False), "ylo")
    mine = lax.dynamic_index_in_dim(ring_a, ylo, 0, keepdims=False)
    return tuple(finish([mine, theirs], got_b))


def solution(mesh):
    fine = Mesh(mesh.devices.reshape(2, 4, 2, 4, 2), DP + TENSOR)
    placed = (
        P(DP, None, TENSOR),
        P(DP, None, TENSOR),
        P(DP, None, TENSOR),
        P(TENSOR, None),
        P(DP, TENSOR, None),
        P(DP, TENSOR),
        P(DP, TENSOR),
        P(DP, TENSOR),
    )
    return jax.shard_map(
        per_device,
        mesh=fine,
        in_specs=placed,
        out_specs=(P(DP, TENSOR), P(DP, TENSOR), P(DP, TENSOR)),
        check_vma=False,
    )
```

```python
import functools

import jax
import jax.numpy as jnp
from jax import lax
from jax.experimental import pallas as pl
from jax.experimental.pallas import tpu as pltpu
from jax.sharding import Mesh, PartitionSpec as P

HEAD = 128
FACTOR = HEAD ** (-0.5)
LOG2E = 1.4426950408889634
BLOCK = 256
SEQ = 1024
DP = ("ylo", "z", "core")
TENSOR = ("x", "yhi")
NT = (((1,), (1,)), ((), ()))
VMEM = pltpu.CompilerParams(vmem_limit_bytes=60 * 1024 * 1024)


def cost(us, moved=0):
    return pl.CostEstimate(flops=int(us * 1.0e9), bytes_accessed=moved, transcendentals=0)


def dot(a, b):
    return jnp.dot(a, b, preferred_element_type=jnp.float32)


def parts_of(number):
    first = number * BLOCK
    own = (first, first + BLOCK)
    return [(0, first), own] if first else [own]


def teacher_kernel(q_ref, k_ref, v_ref, o_ref):
    row = lax.broadcasted_iota(jnp.int32, (BLOCK, BLOCK), 0)
    col = lax.broadcasted_iota(jnp.int32, (BLOCK, BLOCK), 1)
    for number in range(SEQ // BLOCK):
        first = number * BLOCK
        limit = first + BLOCK
        parts = parts_of(number)
        for head in range(2):
            cols = slice(head * HEAD, head * HEAD + HEAD)
            queries = q_ref[first:limit, cols]
            scores = [
                lax.dot_general(queries, k_ref[lo:hi, :], NT, preferred_element_type=jnp.float32)
                for lo, hi in parts
            ]
            scores[-1] = jnp.where(col <= row, scores[-1], -1e30)
            top = functools.reduce(
                jnp.maximum, [jnp.max(s, axis=1, keepdims=True) for s in scores]
            )
            weights = [jnp.exp2((s - top) * (FACTOR * LOG2E)) for s in scores]
            total = sum(jnp.sum(w, axis=1, keepdims=True) for w in weights)
            context = sum(
                dot(w.astype(jnp.bfloat16), v_ref[lo:hi, :]) for w, (lo, hi) in zip(weights, parts)
            )
            o_ref[first:limit, cols] = (context / total).astype(jnp.bfloat16)


def teacher_attention(queries, keys, values, half, before=()):
    steps = queries.shape[1] // (4 * HEAD)
    pair = pl.BlockSpec((SEQ, 2 * HEAD), lambda h: (0, half * steps + h))
    one = pl.BlockSpec((SEQ, HEAD), lambda h: (0, 0))
    return pl.pallas_call(
        lambda q_ref, k_ref, v_ref, *rest: teacher_kernel(q_ref, k_ref, v_ref, rest[-1]),
        grid=(steps,),
        in_specs=[pair, one, one] + [pl.BlockSpec(memory_space=pl.ANY)] * len(before),
        out_specs=pair,
        out_shape=jax.ShapeDtypeStruct(queries.shape, jnp.bfloat16),
        input_output_aliases={3: 0} if before else {},
        compiler_params=VMEM,
        cost_estimate=cost(150 if before else 40),
        name="teacher_attention",
    )(queries, keys, values, *before)


def project_kernel(order_ref, context_ref, a_ref, b_ref, o_ref):
    o_ref[0] = dot(context_ref[...], a_ref[...]).astype(jnp.bfloat16)
    o_ref[1] = dot(context_ref[...], b_ref[...]).astype(jnp.bfloat16)


def project(order, context, projector, weight):
    rows = projector.shape[0]
    count = order.shape[0]
    return pl.pallas_call(
        project_kernel,
        grid_spec=pltpu.PrefetchScalarGridSpec(
            num_scalar_prefetch=1,
            grid=(count // 2,),
            in_specs=[
                pl.BlockSpec(context.shape, lambda g, order: (0, 0)),
                pl.BlockSpec((rows, 256), lambda g, order: (0, order[2 * g])),
                pl.BlockSpec((rows, 256), lambda g, order: (0, order[2 * g + 1])),
            ],
            out_specs=pl.BlockSpec((2, SEQ, 256), lambda g, order: (g, 0, 0)),
        ),
        out_shape=jax.ShapeDtypeStruct((count, SEQ, 256), jnp.bfloat16),
        compiler_params=VMEM,
        cost_estimate=cost(weight),
        name="project",
    )(order, context, projector, projector)


def student_project_kernel(count, *refs):
    at_ref, pieces, near_ref, far_ref = refs[0], refs[2 : 2 + count], refs[2 + count], refs[3 + count]
    o_ref, rows_ref, total = refs[-3:]
    step = pl.program_id(0)
    for number, ref in enumerate(pieces):
        rows_ref[pl.ds(pl.multiple_of(at_ref[number], 64), ref.shape[0]), :] = ref[...]

    @pl.when(step == 0)
    def _():
        total[...] = dot(rows_ref[...], near_ref[...])

    @pl.when(step == 1)
    def _():
        o_ref[...] = (total[...] + dot(rows_ref[...], far_ref[...])).astype(jnp.bfloat16)


def student_project(places, order, pieces, near, far, before=()):
    depth, cols = near.shape
    half = SEQ // 2
    block = depth
    side = 1 if before else 0
    count = len(pieces)
    return pl.pallas_call(
        lambda *refs: student_project_kernel(count, *refs),
        grid_spec=pltpu.PrefetchScalarGridSpec(
            num_scalar_prefetch=2,
            grid=(2,),
            in_specs=[
                pl.BlockSpec((p.shape[0], block), lambda k, at, order: (0, order[k]))
                for p in pieces
            ]
            + [
                pl.BlockSpec((block, cols), lambda k, at, order: (0, 0)),
                pl.BlockSpec((block, cols), lambda k, at, order: (0, 0)),
            ]
            + [pl.BlockSpec(memory_space=pl.ANY)] * len(before),
            out_specs=[
                pl.BlockSpec((half, cols), lambda k, at, order: (side, 0)),
                pl.BlockSpec((half, block), lambda k, at, order: (side, order[k])),
            ],
            scratch_shapes=[pltpu.VMEM((half, cols), jnp.float32)],
        ),
        out_shape=[
            jax.ShapeDtypeStruct((SEQ, cols), jnp.bfloat16),
            jax.ShapeDtypeStruct((SEQ, 2 * depth), jnp.bfloat16),
        ],
        input_output_aliases={4 + count: 0, 5 + count: 1} if before else {},
        compiler_params=VMEM,
        cost_estimate=cost(9 if before else 0),
        name="student_project",
    )(places, order, *pieces, near, far, *before)


def weight_grad_ring_kernel(grad_ref, rows_ref, o_ref):
    product = dot(grad_ref[...], rows_ref[...]).astype(jnp.bfloat16)
    for z in range(2):
        for core in range(2):
            at = (2 * z + core) * 256
            o_ref[z, core, 0] = product[:, at : at + 256]


def weight_grad_ring(grads, rows):
    cols = grads.shape[0]
    return pl.pallas_call(
        weight_grad_ring_kernel,
        grid=(4,),
        in_specs=[
            pl.BlockSpec(grads.shape, lambda k: (0, 0)),
            pl.BlockSpec((SEQ, 1024), lambda k: (0, k)),
        ],
        out_specs=pl.BlockSpec((2, 2, 1, cols, 256), lambda k: (k % 2, 0, k // 2, 0, 0)),
        out_shape=jax.ShapeDtypeStruct((4, 2, 2, cols, 256), jnp.bfloat16),
        compiler_params=VMEM,
        cost_estimate=cost(4),
        name="weight_grad_ring",
    )(grads, rows)


def weight_grad_kernel(core_ref, grad_ref, rows_ref, kept_ref, sent_ref):
    product = dot(grad_ref[...], rows_ref[...]).astype(jnp.bfloat16)

    def store(first, second):
        for z in range(2):
            first[z] = product[:, 512 * z : 512 * z + 256]
            second[z] = product[:, 512 * z + 256 : 512 * z + 512]

    @pl.when(core_ref[0] == 0)
    def _():
        store(kept_ref, sent_ref)

    @pl.when(core_ref[0] == 1)
    def _():
        store(sent_ref, kept_ref)


def weight_grad(core, grads, rows):
    cols = grads.shape[0]
    out = pl.BlockSpec((2, cols, 256), lambda k, core: (k, 0, 0))
    return pl.pallas_call(
        weight_grad_kernel,
        grid_spec=pltpu.PrefetchScalarGridSpec(
            num_scalar_prefetch=1,
            grid=(4,),
            in_specs=[
                pl.BlockSpec(grads.shape, lambda k, core: (0, 0)),
                pl.BlockSpec((SEQ, 1024), lambda k, core: (0, k)),
            ],
            out_specs=[out, out],
        ),
        out_shape=[jax.ShapeDtypeStruct((8, cols, 256), jnp.bfloat16)] * 2,
        compiler_params=VMEM,
        cost_estimate=cost(4),
        name="weight_grad",
    )(core, grads, rows)


def pair_kernel(order_ref, a_ref, b_ref, *outs):
    for number, ref in enumerate(outs):
        at = order_ref[number]
        ref[...] = (a_ref[at].astype(jnp.float32) + b_ref[at].astype(jnp.float32)).astype(
            jnp.bfloat16
        )


def pair_sum(order, a, b):
    whole = pl.BlockSpec(a.shape, lambda i, order: (0, 0, 0))
    one = pl.BlockSpec(a.shape[1:], lambda i, order: (0, 0))
    return pl.pallas_call(
        pair_kernel,
        grid_spec=pltpu.PrefetchScalarGridSpec(
            num_scalar_prefetch=1,
            grid=(1,),
            in_specs=[whole, whole],
            out_specs=[one] * a.shape[0],
        ),
        out_shape=[jax.ShapeDtypeStruct(a.shape[1:], jnp.bfloat16) for _ in range(a.shape[0])],
        compiler_params=VMEM,
        cost_estimate=cost(3),
        name="pair_sum",
    )(order, a, b)


def forward_kernel(y_ref, q_in, k_in, v_in, q_ref, kv_ref, probs_ref, context_ref, vt):
    y = y_ref[0]
    for block in range(4):
        for which, side in ((0, y), (1, 1 - y)):
            rows = slice((4 * which + block) * HEAD, (4 * which + block) * HEAD + HEAD)
            at = pl.ds(pl.multiple_of((2 * block + side) * HEAD, HEAD), HEAD)
            q_ref[at, :] = q_in[rows, :]
            kv_ref[at, :HEAD] = k_in[rows, :]
            kv_ref[at, HEAD:] = v_in[rows, :]
    vt[...] = kv_ref[:, HEAD:].T
    key = lax.broadcasted_iota(jnp.int32, (BLOCK, BLOCK), 0)
    query = lax.broadcasted_iota(jnp.int32, (BLOCK, BLOCK), 1)
    for number in range(SEQ // BLOCK):
        first = number * BLOCK
        limit = first + BLOCK
        parts = parts_of(number)
        for head in range(2):
            cols = slice(head * HEAD, head * HEAD + HEAD)
            queries = q_ref[first:limit, cols]
            scores = [
                lax.dot_general(
                    kv_ref[lo:hi, :HEAD], queries, NT, preferred_element_type=jnp.float32
                )
                for lo, hi in parts
            ]
            scores[-1] = jnp.where(key <= query, scores[-1], -1e30)
            top = functools.reduce(
                jnp.maximum, [jnp.max(s, axis=0, keepdims=True) for s in scores]
            )
            weights = [jnp.exp2((s - top) * (FACTOR * LOG2E)) for s in scores]
            scale = 1.0 / sum(jnp.sum(w, axis=0, keepdims=True) for w in weights)
            context = 0.0
            for w, (lo, hi) in zip(weights, parts):
                rounded = (w * scale).astype(jnp.bfloat16)
                probs_ref[head, lo:hi, first:limit] = rounded
                context += dot(vt[:, lo:hi], rounded)
            context_ref[first:limit, cols] = context.T


def student_forward(y, projected):
    pair = pl.BlockSpec((SEQ, 2 * HEAD), lambda i, y: (0, i))
    both = pl.BlockSpec((SEQ, 2 * HEAD), lambda i, y: (0, 0))
    return pl.pallas_call(
        forward_kernel,
        grid_spec=pltpu.PrefetchScalarGridSpec(
            num_scalar_prefetch=1,
            grid=(2,),
            in_specs=[
                pair,
                pl.BlockSpec((SEQ, HEAD), lambda i, y: (0, 4)),
                pl.BlockSpec((SEQ, HEAD), lambda i, y: (0, 5)),
            ],
            out_specs=[pair, both, pl.BlockSpec((2, SEQ, SEQ), lambda i, y: (i, 0, 0)), pair],
            scratch_shapes=[pltpu.VMEM((HEAD, SEQ), jnp.bfloat16)],
        ),
        out_shape=[
            jax.ShapeDtypeStruct((SEQ, 4 * HEAD), jnp.bfloat16),
            jax.ShapeDtypeStruct((SEQ, 2 * HEAD), jnp.bfloat16),
            jax.ShapeDtypeStruct((4, SEQ, SEQ), jnp.bfloat16),
            jax.ShapeDtypeStruct((SEQ, 4 * HEAD), jnp.float32),
        ],
        compiler_params=VMEM,
        cost_estimate=cost(60),
        name="student_forward",
    )(y, projected, projected, projected)


def backward_kernel(count, has_start, y_ref, q_ref, kv_ref, probs_ref, context_ref, *rest):
    targets, rest = rest[:count], rest[count:]
    if has_start:
        start_ref, grad_ref, kt, dk, dv = rest
        dk[...] = start_ref[:, :HEAD]
        dv[...] = start_ref[:, HEAD:]
    else:
        grad_ref, gkv_ref, kt, dk, dv = rest
        dk[...] = jnp.zeros_like(dk)
        dv[...] = jnp.zeros_like(dv)
    y = y_ref[0]
    kt[...] = kv_ref[:, :HEAD].T

    def store(at, block, value):
        for which, side in ((0, y), (1, 1 - y)):
            lanes = pl.ds(pl.multiple_of((4 * side + block) * HEAD, HEAD), HEAD)
            grad_ref[at, lanes] = value[:, which * HEAD : which * HEAD + HEAD]

    for number in range(SEQ // BLOCK):
        first = number * BLOCK
        limit = first + BLOCK
        parts = parts_of(number)
        for head in range(2):
            cols = slice(head * HEAD, head * HEAD + HEAD)
            queries = q_ref[first:limit, cols]
            target = 0.0
            for part in targets:
                target += part[0, first:limit, cols].astype(jnp.float32)
            incoming = ((context_ref[first:limit, cols] - target) * (1.0 / 16)).astype(
                jnp.bfloat16
            )
            rounded = [probs_ref[head, lo:hi, first:limit] for lo, hi in parts]
            probs = [r.astype(jnp.float32) for r in rounded]
            grad_probs = [
                lax.dot_general(
                    kv_ref[lo:hi, HEAD:], incoming, NT, preferred_element_type=jnp.float32
                )
                for lo, hi in parts
            ]
            inner = sum(
                jnp.sum(g * p, axis=0, keepdims=True) for g, p in zip(grad_probs, probs)
            )
            scaled = [
                (p * (g - inner)).astype(jnp.bfloat16) for g, p in zip(grad_probs, probs)
            ]
            for r, s, (lo, hi) in zip(rounded, scaled, parts):
                dv[lo:hi, :] += dot(r, incoming)
                dk[lo:hi, :] += dot(s, queries)
            grad = sum(dot(kt[:, lo:hi], s) for s, (lo, hi) in zip(scaled, parts))
            store(cols, number, (grad * FACTOR).astype(jnp.bfloat16))

    if has_start:
        for number in range(SEQ // BLOCK):
            rows = slice(number * BLOCK, number * BLOCK + BLOCK)
            store(slice(256, 384), number, (dk[rows, :] * FACTOR).T.astype(jnp.bfloat16))
            store(slice(384, 512), number, dv[rows, :].T.astype(jnp.bfloat16))
    else:
        gkv_ref[:, :HEAD] = dk[...]
        gkv_ref[:, HEAD:] = dv[...]


def student_backward(y, forward, targets, part, start=None):
    queries, kv, probs, context = forward
    pair = pl.BlockSpec((SEQ, 2 * HEAD), lambda i, y: (0, part))
    whole = pl.BlockSpec((SEQ, 2 * HEAD), lambda i, y: (0, 0))
    columns = 256 if start is None else 512
    grad = pl.BlockSpec((columns, SEQ), lambda i, y: (0, 0))
    grad_shape = jax.ShapeDtypeStruct((columns, SEQ), jnp.bfloat16)
    at_side = pl.BlockSpec((1, SEQ, 2 * HEAD), lambda i, y: (y[0], 0, 0))
    alone = pl.BlockSpec((1, SEQ, 2 * HEAD), lambda i, y: (0, 0, 0))
    return pl.pallas_call(
        lambda *refs: backward_kernel(len(targets), start is not None, *refs),
        grid_spec=pltpu.PrefetchScalarGridSpec(
            num_scalar_prefetch=1,
            grid=(1,),
            in_specs=[pair, whole, pl.BlockSpec((2, SEQ, SEQ), lambda i, y: (part, 0, 0)), pair]
            + [alone if t.shape[0] == 1 else at_side for t in targets]
            + [whole] * (start is not None),
            out_specs=[grad, whole] if start is None else [grad],
            scratch_shapes=[
                pltpu.VMEM((HEAD, SEQ), jnp.bfloat16),
                pltpu.VMEM((SEQ, HEAD), jnp.float32),
                pltpu.VMEM((SEQ, HEAD), jnp.float32),
            ],
        ),
        out_shape=[grad_shape, jax.ShapeDtypeStruct((SEQ, 2 * HEAD), jnp.float32)]
        if start is None
        else [grad_shape],
        compiler_params=VMEM,
        cost_estimate=cost(8),
        name="student_backward",
    )(y, queries, kv, probs, context, *targets, *([] if start is None else [start]))


def shift(array, axis, step=1):
    n = lax.axis_size(axis)
    return lax.ppermute(array, axis, [(i, (i + step) % n) for i in range(n)])


def gather_rows_near(own):
    return shift(own, "yhi"), shift(own, "x", 1), shift(own, "x", -1)


def far_halves(left, right):
    half = left.shape[0] // 2
    return shift(left[:half], "x", 1), shift(right[half:], "x", -1)


def row_places(x):
    places = [(x + dx) % 4 * 128 + offset for dx, offset in ((0, 0), (3, 0), (1, 0), (2, 0), (2, 64))]
    return jnp.stack(places).astype(jnp.int32)


RELATIVE = [(dy, dz) for dy in range(2) for dz in range(4)]


def row_blocks():
    y = lax.axis_index("ylo")
    z = lax.axis_index("z")
    return jnp.stack([(y + dy) % 2 * 4 + (z + dz) % 4 for dy, dz in RELATIVE]).astype(jnp.int32)


def send_direct(blocks):
    got = [blocks[0]]
    for (dy, dz), block in zip(RELATIVE[1:], blocks[1:]):
        route = [(i * 4 + k, (i + dy) % 2 * 4 + (k + dz) % 4) for i in range(2) for k in range(4)]
        got.append(lax.ppermute(block, ("ylo", "z"), route))
    return got


def finish_kernel(*refs):
    a_refs, b_refs, (q_ref, k_ref, v_ref) = refs[:2], refs[2:10], refs[10:]

    def total(parts):
        result = parts[0][...].astype(jnp.float32)
        for part in parts[1:]:
            result += part[...].astype(jnp.float32)
        return result.T

    q_ref[:, :256] = total(a_refs)
    rest = total(b_refs)
    q_ref[:, 256:] = rest[:, :256]
    k_ref[...] = rest[:, 256:384]
    v_ref[...] = rest[:, 384:]


def finish(got_a, got_b):
    return pl.pallas_call(
        finish_kernel,
        out_shape=[jax.ShapeDtypeStruct((256, cols), jnp.float32) for cols in (512, 128, 128)],
        compiler_params=VMEM,
        cost_estimate=cost(3),
        name="finish",
    )(*got_a, *got_b)


def per_device(
    teacher_queries,
    teacher_keys,
    teacher_values,
    projector,
    student_inputs,
    query_weight,
    key_weight,
    value_weight,
):
    tq, tk, tv = teacher_queries[0], teacher_keys[0], teacher_values[0]
    x, yhi, ylo = lax.axis_index("x"), lax.axis_index("yhi"), lax.axis_index("ylo")
    own = student_inputs[0]
    other, left, right = gather_rows_near(own)

    groups = jnp.arange(4, dtype=jnp.int32)
    context = teacher_attention(tq, tk, tv, 0)
    context, query_weight, key_weight, value_weight = lax.optimization_barrier(
        (context, query_weight, key_weight, value_weight)
    )
    shard = jnp.concatenate([query_weight, key_weight, value_weight], axis=1)
    near = lax.all_gather(shard, ("z", "core"), axis=0, tiled=True)
    shard_far = shift(shard, "ylo")
    context = teacher_attention(tq, tk, tv, 1, (context,))
    sent = project(2 * (2 * groups + 1 - yhi), context, projector, 0)
    context, left, right, other, sent, shard_far = lax.optimization_barrier(
        (context, left, right, other, sent, shard_far)
    )
    far = lax.all_gather(shard_far, ("z", "core"), axis=0, tiled=True)
    came = shift(sent, "yhi")
    own_far = far_halves(left, right)
    other_left, other_right = shift(other, "x", 1), shift(other, "x", -1)

    product_b = project(2 * jnp.arange(8, dtype=jnp.int32) + 1, context, projector, 0)
    sum_b = lax.psum_scatter(product_b, "x", scatter_dimension=0, tiled=True)
    context, other_left, other_right, own_far, product_b = lax.optimization_barrier(
        (context, other_left, other_right, own_far, product_b)
    )
    kept = project(2 * (2 * groups + yhi), context, projector, 30)
    other_far = far_halves(other_left, other_right)

    places = row_places(x)
    order = jnp.stack([ylo, 1 - ylo]).astype(jnp.int32)
    before = student_project(places, order, [own, left, right, *own_far], near, far)
    came, before = lax.optimization_barrier((came, before))
    by_x = ((x + jnp.arange(4)) % 4).astype(jnp.int32)
    blocks_a = pair_sum(by_x, kept, came)
    targets_a = [blocks_a[0][None]] + [
        shift(block, "x", step)[None] for step, block in enumerate(blocks_a) if step
    ]
    projected, rows = student_project(
        places, order, [other, other_left, other_right, *other_far], near, far, before
    )

    y = yhi.astype(jnp.int32).reshape(1)
    core = lax.axis_index("core").astype(jnp.int32).reshape(1)
    forward = student_forward(y, projected)
    sum_b, forward = lax.optimization_barrier((sum_b, forward))
    theirs_b = shift(lax.dynamic_slice_in_dim(sum_b, 1 - yhi, 1, 0), "yhi")
    forward, targets_a = lax.optimization_barrier((forward, targets_a))

    grad_a, part_kv = student_backward(y, forward, targets_a, 0)
    theirs_b, grad_a = lax.optimization_barrier((theirs_b, grad_a))
    whole_a = weight_grad_ring(grad_a, rows)
    ring_a = lax.psum_scatter(
        whole_a.reshape(16, 256, 256), ("z", "core"), scatter_dimension=0, tiled=True
    )
    theirs_b, whole_a = lax.optimization_barrier((theirs_b, whole_a))
    (grad_b,) = student_backward(y, forward, [sum_b, theirs_b], 1, start=part_kv)
    kept_b, sent_b = weight_grad(core, grad_b, rows)
    got_b = send_direct(list(pair_sum(row_blocks(), kept_b, shift(sent_b, "core"))))
    theirs = shift(lax.dynamic_index_in_dim(ring_a, 1 - ylo, 0, keepdims=False), "ylo")
    mine = lax.dynamic_index_in_dim(ring_a, ylo, 0, keepdims=False)
    return tuple(finish([mine, theirs], got_b))


def solution(mesh):
    fine = Mesh(mesh.devices.reshape(2, 4, 2, 4, 2), DP + TENSOR)
    placed = (
        P(DP, None, TENSOR),
        P(DP, None, TENSOR),
        P(DP, None, TENSOR),
        P(TENSOR, None),
        P(DP, TENSOR, None),
        P(DP, TENSOR),
        P(DP, TENSOR),
        P(DP, TENSOR),
    )
    return jax.shard_map(
        per_device,
        mesh=fine,
        in_specs=placed,
        out_specs=(P(DP, TENSOR), P(DP, TENSOR), P(DP, TENSOR)),
        check_vma=False,
    )
```

```python
import functools

import jax
import jax.numpy as jnp
from jax import lax
from jax.experimental import pallas as pl
from jax.experimental.pallas import tpu as pltpu
from jax.sharding import Mesh, PartitionSpec as P

HEAD = 128
FACTOR = HEAD ** (-0.5)
LOG2E = 1.4426950408889634
BLOCK = 256
SEQ = 1024
DP = ("ylo", "z", "core")
TENSOR = ("x", "yhi")
NT = (((1,), (1,)), ((), ()))
VMEM = pltpu.CompilerParams(vmem_limit_bytes=60 * 1024 * 1024)


def cost(us, moved=0):
    return pl.CostEstimate(flops=int(us * 1.0e9), bytes_accessed=moved, transcendentals=0)


def dot(a, b):
    return jnp.dot(a, b, preferred_element_type=jnp.float32)


def parts_of(number):
    first = number * BLOCK
    own = (first, first + BLOCK)
    return [(0, first), own] if first else [own]


def teacher_kernel(q_ref, k_ref, v_ref, o_ref):
    row = lax.broadcasted_iota(jnp.int32, (BLOCK, BLOCK), 0)
    col = lax.broadcasted_iota(jnp.int32, (BLOCK, BLOCK), 1)
    for number in range(SEQ // BLOCK):
        first = number * BLOCK
        limit = first + BLOCK
        parts = parts_of(number)
        for head in range(2):
            cols = slice(head * HEAD, head * HEAD + HEAD)
            queries = q_ref[first:limit, cols]
            scores = [
                lax.dot_general(queries, k_ref[lo:hi, :], NT, preferred_element_type=jnp.float32)
                for lo, hi in parts
            ]
            scores[-1] = jnp.where(col <= row, scores[-1], -1e30)
            top = functools.reduce(
                jnp.maximum, [jnp.max(s, axis=1, keepdims=True) for s in scores]
            )
            weights = [jnp.exp2((s - top) * (FACTOR * LOG2E)) for s in scores]
            total = sum(jnp.sum(w, axis=1, keepdims=True) for w in weights)
            context = sum(
                dot(w.astype(jnp.bfloat16), v_ref[lo:hi, :]) for w, (lo, hi) in zip(weights, parts)
            )
            o_ref[first:limit, cols] = (context / total).astype(jnp.bfloat16)


def teacher_attention(queries, keys, values, half, before=()):
    steps = queries.shape[1] // (4 * HEAD)
    pair = pl.BlockSpec((SEQ, 2 * HEAD), lambda h: (0, half * steps + h))
    one = pl.BlockSpec((SEQ, HEAD), lambda h: (0, 0))
    return pl.pallas_call(
        lambda q_ref, k_ref, v_ref, *rest: teacher_kernel(q_ref, k_ref, v_ref, rest[-1]),
        grid=(steps,),
        in_specs=[pair, one, one] + [pl.BlockSpec(memory_space=pl.ANY)] * len(before),
        out_specs=pair,
        out_shape=jax.ShapeDtypeStruct(queries.shape, jnp.bfloat16),
        input_output_aliases={3: 0} if before else {},
        compiler_params=VMEM,
        cost_estimate=cost(150 if before else 40),
        name="teacher_attention",
    )(queries, keys, values, *before)


def project_kernel(order_ref, context_ref, a_ref, b_ref, o_ref):
    o_ref[0] = dot(context_ref[...], a_ref[...]).astype(jnp.bfloat16)
    o_ref[1] = dot(context_ref[...], b_ref[...]).astype(jnp.bfloat16)


def project(order, context, projector, weight):
    rows = projector.shape[0]
    count = order.shape[0]
    return pl.pallas_call(
        project_kernel,
        grid_spec=pltpu.PrefetchScalarGridSpec(
            num_scalar_prefetch=1,
            grid=(count // 2,),
            in_specs=[
                pl.BlockSpec(context.shape, lambda g, order: (0, 0)),
                pl.BlockSpec((rows, 256), lambda g, order: (0, order[2 * g])),
                pl.BlockSpec((rows, 256), lambda g, order: (0, order[2 * g + 1])),
            ],
            out_specs=pl.BlockSpec((2, SEQ, 256), lambda g, order: (g, 0, 0)),
        ),
        out_shape=jax.ShapeDtypeStruct((count, SEQ, 256), jnp.bfloat16),
        compiler_params=VMEM,
        cost_estimate=cost(weight),
        name="project",
    )(order, context, projector, projector)


def student_project_kernel(count, *refs):
    at_ref, pieces, near_ref, far_ref = refs[0], refs[2 : 2 + count], refs[2 + count], refs[3 + count]
    o_ref, rows_ref, total = refs[-3:]
    step = pl.program_id(0)
    for number, ref in enumerate(pieces):
        rows_ref[pl.ds(pl.multiple_of(at_ref[number], 64), ref.shape[0]), :] = ref[...]

    @pl.when(step == 0)
    def _():
        total[...] = dot(rows_ref[...], near_ref[...])

    @pl.when(step == 1)
    def _():
        o_ref[...] = (total[...] + dot(rows_ref[...], far_ref[...])).astype(jnp.bfloat16)


def student_project(places, order, pieces, near, far, before=()):
    depth, cols = near.shape
    half = SEQ // 2
    block = depth
    side = 1 if before else 0
    count = len(pieces)
    return pl.pallas_call(
        lambda *refs: student_project_kernel(count, *refs),
        grid_spec=pltpu.PrefetchScalarGridSpec(
            num_scalar_prefetch=2,
            grid=(2,),
            in_specs=[
                pl.BlockSpec((p.shape[0], block), lambda k, at, order: (0, order[k]))
                for p in pieces
            ]
            + [
                pl.BlockSpec((block, cols), lambda k, at, order: (0, 0)),
                pl.BlockSpec((block, cols), lambda k, at, order: (0, 0)),
            ]
            + [pl.BlockSpec(memory_space=pl.ANY)] * len(before),
            out_specs=[
                pl.BlockSpec((half, cols), lambda k, at, order: (side, 0)),
                pl.BlockSpec((half, block), lambda k, at, order: (side, order[k])),
            ],
            scratch_shapes=[pltpu.VMEM((half, cols), jnp.float32)],
        ),
        out_shape=[
            jax.ShapeDtypeStruct((SEQ, cols), jnp.bfloat16),
            jax.ShapeDtypeStruct((SEQ, 2 * depth), jnp.bfloat16),
        ],
        input_output_aliases={4 + count: 0, 5 + count: 1} if before else {},
        compiler_params=VMEM,
        cost_estimate=cost(9 if before else 0),
        name="student_project",
    )(places, order, *pieces, near, far, *before)


def weight_grad_ring_kernel(grad_ref, rows_ref, o_ref):
    product = dot(grad_ref[...], rows_ref[...]).astype(jnp.bfloat16)
    for z in range(2):
        for core in range(2):
            at = (2 * z + core) * 256
            o_ref[z, core, 0] = product[:, at : at + 256]


def weight_grad_ring(grads, rows):
    cols = grads.shape[0]
    return pl.pallas_call(
        weight_grad_ring_kernel,
        grid=(4,),
        in_specs=[
            pl.BlockSpec(grads.shape, lambda k: (0, 0)),
            pl.BlockSpec((SEQ, 1024), lambda k: (0, k)),
        ],
        out_specs=pl.BlockSpec((2, 2, 1, cols, 256), lambda k: (k % 2, 0, k // 2, 0, 0)),
        out_shape=jax.ShapeDtypeStruct((4, 2, 2, cols, 256), jnp.bfloat16),
        compiler_params=VMEM,
        cost_estimate=cost(4),
        name="weight_grad_ring",
    )(grads, rows)


def weight_grad_kernel(core_ref, grad_ref, rows_ref, kept_ref, sent_ref):
    product = dot(grad_ref[...], rows_ref[...]).astype(jnp.bfloat16)

    def store(first, second):
        for z in range(2):
            first[z] = product[:, 512 * z : 512 * z + 256]
            second[z] = product[:, 512 * z + 256 : 512 * z + 512]

    @pl.when(core_ref[0] == 0)
    def _():
        store(kept_ref, sent_ref)

    @pl.when(core_ref[0] == 1)
    def _():
        store(sent_ref, kept_ref)


def weight_grad(core, grads, rows):
    cols = grads.shape[0]
    out = pl.BlockSpec((2, cols, 256), lambda k, core: (k, 0, 0))
    return pl.pallas_call(
        weight_grad_kernel,
        grid_spec=pltpu.PrefetchScalarGridSpec(
            num_scalar_prefetch=1,
            grid=(4,),
            in_specs=[
                pl.BlockSpec(grads.shape, lambda k, core: (0, 0)),
                pl.BlockSpec((SEQ, 1024), lambda k, core: (0, k)),
            ],
            out_specs=[out, out],
        ),
        out_shape=[jax.ShapeDtypeStruct((8, cols, 256), jnp.bfloat16)] * 2,
        compiler_params=VMEM,
        cost_estimate=cost(4),
        name="weight_grad",
    )(core, grads, rows)


def pair_kernel(order_ref, a_ref, b_ref, *outs):
    for number, ref in enumerate(outs):
        at = order_ref[number]
        ref[...] = (a_ref[at].astype(jnp.float32) + b_ref[at].astype(jnp.float32)).astype(
            jnp.bfloat16
        )


def pair_sum(order, a, b):
    whole = pl.BlockSpec(a.shape, lambda i, order: (0, 0, 0))
    one = pl.BlockSpec(a.shape[1:], lambda i, order: (0, 0))
    return pl.pallas_call(
        pair_kernel,
        grid_spec=pltpu.PrefetchScalarGridSpec(
            num_scalar_prefetch=1,
            grid=(1,),
            in_specs=[whole, whole],
            out_specs=[one] * a.shape[0],
        ),
        out_shape=[jax.ShapeDtypeStruct(a.shape[1:], jnp.bfloat16) for _ in range(a.shape[0])],
        compiler_params=VMEM,
        cost_estimate=cost(3),
        name="pair_sum",
    )(order, a, b)


def forward_kernel(y_ref, q_in, k_in, v_in, q_ref, kv_ref, probs_ref, context_ref, vt):
    y = y_ref[0]
    for block in range(4):
        for which, side in ((0, y), (1, 1 - y)):
            rows = slice((4 * which + block) * HEAD, (4 * which + block) * HEAD + HEAD)
            at = pl.ds(pl.multiple_of((2 * block + side) * HEAD, HEAD), HEAD)
            q_ref[at, :] = q_in[rows, :]
            kv_ref[at, :HEAD] = k_in[rows, :]
            kv_ref[at, HEAD:] = v_in[rows, :]
    vt[...] = kv_ref[:, HEAD:].T
    key = lax.broadcasted_iota(jnp.int32, (BLOCK, BLOCK), 0)
    query = lax.broadcasted_iota(jnp.int32, (BLOCK, BLOCK), 1)
    for number in range(SEQ // BLOCK):
        first = number * BLOCK
        limit = first + BLOCK
        parts = parts_of(number)
        for head in range(2):
            cols = slice(head * HEAD, head * HEAD + HEAD)
            queries = q_ref[first:limit, cols]
            scores = [
                lax.dot_general(
                    kv_ref[lo:hi, :HEAD], queries, NT, preferred_element_type=jnp.float32
                )
                for lo, hi in parts
            ]
            scores[-1] = jnp.where(key <= query, scores[-1], -1e30)
            top = functools.reduce(
                jnp.maximum, [jnp.max(s, axis=0, keepdims=True) for s in scores]
            )
            weights = [jnp.exp2((s - top) * (FACTOR * LOG2E)) for s in scores]
            scale = 1.0 / sum(jnp.sum(w, axis=0, keepdims=True) for w in weights)
            context = 0.0
            for w, (lo, hi) in zip(weights, parts):
                rounded = (w * scale).astype(jnp.bfloat16)
                probs_ref[head, lo:hi, first:limit] = rounded
                context += dot(vt[:, lo:hi], rounded)
            context_ref[first:limit, cols] = context.T


def student_forward(y, projected):
    pair = pl.BlockSpec((SEQ, 2 * HEAD), lambda i, y: (0, i))
    both = pl.BlockSpec((SEQ, 2 * HEAD), lambda i, y: (0, 0))
    return pl.pallas_call(
        forward_kernel,
        grid_spec=pltpu.PrefetchScalarGridSpec(
            num_scalar_prefetch=1,
            grid=(2,),
            in_specs=[
                pair,
                pl.BlockSpec((SEQ, HEAD), lambda i, y: (0, 4)),
                pl.BlockSpec((SEQ, HEAD), lambda i, y: (0, 5)),
            ],
            out_specs=[pair, both, pl.BlockSpec((2, SEQ, SEQ), lambda i, y: (i, 0, 0)), pair],
            scratch_shapes=[pltpu.VMEM((HEAD, SEQ), jnp.bfloat16)],
        ),
        out_shape=[
            jax.ShapeDtypeStruct((SEQ, 4 * HEAD), jnp.bfloat16),
            jax.ShapeDtypeStruct((SEQ, 2 * HEAD), jnp.bfloat16),
            jax.ShapeDtypeStruct((4, SEQ, SEQ), jnp.bfloat16),
            jax.ShapeDtypeStruct((SEQ, 4 * HEAD), jnp.float32),
        ],
        compiler_params=VMEM,
        cost_estimate=cost(60),
        name="student_forward",
    )(y, projected, projected, projected)


def backward_kernel(count, has_start, y_ref, q_ref, kv_ref, probs_ref, context_ref, *rest):
    targets, rest = rest[:count], rest[count:]
    if has_start:
        start_ref, grad_ref, kt, dk, dv = rest
        dk[...] = start_ref[:, :HEAD]
        dv[...] = start_ref[:, HEAD:]
    else:
        grad_ref, gkv_ref, kt, dk, dv = rest
        dk[...] = jnp.zeros_like(dk)
        dv[...] = jnp.zeros_like(dv)
    y = y_ref[0]
    kt[...] = kv_ref[:, :HEAD].T

    def store(at, block, value):
        for which, side in ((0, y), (1, 1 - y)):
            lanes = pl.ds(pl.multiple_of((4 * side + block) * HEAD, HEAD), HEAD)
            grad_ref[at, lanes] = value[:, which * HEAD : which * HEAD + HEAD]

    for number in range(SEQ // BLOCK):
        first = number * BLOCK
        limit = first + BLOCK
        parts = parts_of(number)
        for head in range(2):
            cols = slice(head * HEAD, head * HEAD + HEAD)
            queries = q_ref[first:limit, cols]
            target = 0.0
            for part in targets:
                target += part[0, first:limit, cols].astype(jnp.float32)
            incoming = ((context_ref[first:limit, cols] - target) * (1.0 / 16)).astype(
                jnp.bfloat16
            )
            rounded = [probs_ref[head, lo:hi, first:limit] for lo, hi in parts]
            probs = [r.astype(jnp.float32) for r in rounded]
            grad_probs = [
                lax.dot_general(
                    kv_ref[lo:hi, HEAD:], incoming, NT, preferred_element_type=jnp.float32
                )
                for lo, hi in parts
            ]
            inner = sum(
                jnp.sum(g * p, axis=0, keepdims=True) for g, p in zip(grad_probs, probs)
            )
            scaled = [
                (p * (g - inner)).astype(jnp.bfloat16) for g, p in zip(grad_probs, probs)
            ]
            for r, s, (lo, hi) in zip(rounded, scaled, parts):
                dv[lo:hi, :] += dot(r, incoming)
                dk[lo:hi, :] += dot(s, queries)
            grad = sum(dot(kt[:, lo:hi], s) for s, (lo, hi) in zip(scaled, parts))
            store(cols, number, (grad * FACTOR).astype(jnp.bfloat16))

    if has_start:
        for number in range(SEQ // BLOCK):
            rows = slice(number * BLOCK, number * BLOCK + BLOCK)
            store(slice(256, 384), number, (dk[rows, :] * FACTOR).T.astype(jnp.bfloat16))
            store(slice(384, 512), number, dv[rows, :].T.astype(jnp.bfloat16))
    else:
        gkv_ref[:, :HEAD] = dk[...]
        gkv_ref[:, HEAD:] = dv[...]


def student_backward(y, forward, targets, part, start=None):
    queries, kv, probs, context = forward
    pair = pl.BlockSpec((SEQ, 2 * HEAD), lambda i, y: (0, part))
    whole = pl.BlockSpec((SEQ, 2 * HEAD), lambda i, y: (0, 0))
    columns = 256 if start is None else 512
    grad = pl.BlockSpec((columns, SEQ), lambda i, y: (0, 0))
    grad_shape = jax.ShapeDtypeStruct((columns, SEQ), jnp.bfloat16)
    at_side = pl.BlockSpec((1, SEQ, 2 * HEAD), lambda i, y: (y[0], 0, 0))
    alone = pl.BlockSpec((1, SEQ, 2 * HEAD), lambda i, y: (0, 0, 0))
    return pl.pallas_call(
        lambda *refs: backward_kernel(len(targets), start is not None, *refs),
        grid_spec=pltpu.PrefetchScalarGridSpec(
            num_scalar_prefetch=1,
            grid=(1,),
            in_specs=[pair, whole, pl.BlockSpec((2, SEQ, SEQ), lambda i, y: (part, 0, 0)), pair]
            + [alone if t.shape[0] == 1 else at_side for t in targets]
            + [whole] * (start is not None),
            out_specs=[grad, whole] if start is None else [grad],
            scratch_shapes=[
                pltpu.VMEM((HEAD, SEQ), jnp.bfloat16),
                pltpu.VMEM((SEQ, HEAD), jnp.float32),
                pltpu.VMEM((SEQ, HEAD), jnp.float32),
            ],
        ),
        out_shape=[grad_shape, jax.ShapeDtypeStruct((SEQ, 2 * HEAD), jnp.float32)]
        if start is None
        else [grad_shape],
        compiler_params=VMEM,
        cost_estimate=cost(8),
        name="student_backward",
    )(y, queries, kv, probs, context, *targets, *([] if start is None else [start]))


def shift(array, axis, step=1):
    n = lax.axis_size(axis)
    return lax.ppermute(array, axis, [(i, (i + step) % n) for i in range(n)])


def gather_rows_near(own):
    return shift(own, "yhi"), shift(own, "x", 1), shift(own, "x", -1)


def far_halves(left, right):
    half = left.shape[0] // 2
    return shift(left[:half], "x", 1), shift(right[half:], "x", -1)


def row_places(x):
    places = [(x + dx) % 4 * 128 + offset for dx, offset in ((0, 0), (3, 0), (1, 0), (2, 0), (2, 64))]
    return jnp.stack(places).astype(jnp.int32)


RELATIVE = [(0, 0), (0, 2), (1, 2), (1, 1), (1, 3), (1, 0), (0, 1), (0, 3)]


def row_blocks():
    y = lax.axis_index("ylo")
    z = lax.axis_index("z")
    return jnp.stack([(y + dy) % 2 * 4 + (z + dz) % 4 for dy, dz in RELATIVE]).astype(jnp.int32)


def send_direct(blocks):
    got = [blocks[0]]
    for (dy, dz), block in zip(RELATIVE[1:], blocks[1:]):
        route = [(i * 4 + k, (i + dy) % 2 * 4 + (k + dz) % 4) for i in range(2) for k in range(4)]
        got.append(lax.ppermute(block, ("ylo", "z"), route))
    return got


def finish_kernel(*refs):
    a_refs, b_refs, (q_ref, k_ref, v_ref) = refs[:2], refs[2:10], refs[10:]

    def total(parts):
        result = parts[0][...].astype(jnp.float32)
        for part in parts[1:]:
            result += part[...].astype(jnp.float32)
        return result.T

    q_ref[:, :256] = total(a_refs)
    rest = total(b_refs)
    q_ref[:, 256:] = rest[:, :256]
    k_ref[...] = rest[:, 256:384]
    v_ref[...] = rest[:, 384:]


def finish(got_a, got_b):
    return pl.pallas_call(
        finish_kernel,
        out_shape=[jax.ShapeDtypeStruct((256, cols), jnp.float32) for cols in (512, 128, 128)],
        compiler_params=VMEM,
        cost_estimate=cost(3),
        name="finish",
    )(*got_a, *got_b)


def per_device(
    teacher_queries,
    teacher_keys,
    teacher_values,
    projector,
    student_inputs,
    query_weight,
    key_weight,
    value_weight,
):
    tq, tk, tv = teacher_queries[0], teacher_keys[0], teacher_values[0]
    x, yhi, ylo = lax.axis_index("x"), lax.axis_index("yhi"), lax.axis_index("ylo")
    own = student_inputs[0]
    other, left, right = gather_rows_near(own)

    groups = jnp.arange(4, dtype=jnp.int32)
    context = teacher_attention(tq, tk, tv, 0)
    context, query_weight, key_weight, value_weight = lax.optimization_barrier(
        (context, query_weight, key_weight, value_weight)
    )
    shard = jnp.concatenate([query_weight, key_weight, value_weight], axis=1)
    near = lax.all_gather(shard, ("z", "core"), axis=0, tiled=True)
    shard_far = shift(shard, "ylo")
    context = teacher_attention(tq, tk, tv, 1, (context,))
    sent = project(2 * (2 * groups + 1 - yhi), context, projector, 0)
    context, left, right, other, sent, shard_far = lax.optimization_barrier(
        (context, left, right, other, sent, shard_far)
    )
    far = lax.all_gather(shard_far, ("z", "core"), axis=0, tiled=True)
    came = shift(sent, "yhi")
    own_far = far_halves(left, right)
    other_left, other_right = shift(other, "x", 1), shift(other, "x", -1)

    product_b = project(2 * jnp.arange(8, dtype=jnp.int32) + 1, context, projector, 0)
    sum_b = lax.psum_scatter(product_b, "x", scatter_dimension=0, tiled=True)
    context, other_left, other_right, own_far, product_b = lax.optimization_barrier(
        (context, other_left, other_right, own_far, product_b)
    )
    kept = project(2 * (2 * groups + yhi), context, projector, 30)
    other_far = far_halves(other_left, other_right)

    places = row_places(x)
    order = jnp.stack([ylo, 1 - ylo]).astype(jnp.int32)
    before = student_project(places, order, [own, left, right, *own_far], near, far)
    came, before = lax.optimization_barrier((came, before))
    by_x = ((x + jnp.arange(4)) % 4).astype(jnp.int32)
    blocks_a = pair_sum(by_x, kept, came)
    targets_a = [blocks_a[0][None]] + [
        shift(block, "x", step)[None] for step, block in enumerate(blocks_a) if step
    ]
    projected, rows = student_project(
        places, order, [other, other_left, other_right, *other_far], near, far, before
    )

    y = yhi.astype(jnp.int32).reshape(1)
    core = lax.axis_index("core").astype(jnp.int32).reshape(1)
    forward = student_forward(y, projected)
    forward, targets_a = lax.optimization_barrier((forward, targets_a))

    grad_a, part_kv = student_backward(y, forward, targets_a, 0)
    sum_b, grad_a = lax.optimization_barrier((sum_b, grad_a))
    theirs_b = shift(lax.dynamic_slice_in_dim(sum_b, 1 - yhi, 1, 0), "yhi")
    whole_a = weight_grad_ring(grad_a, rows)
    ring_a = lax.psum_scatter(
        whole_a.reshape(16, 256, 256), ("z", "core"), scatter_dimension=0, tiled=True
    )
    theirs_b, whole_a = lax.optimization_barrier((theirs_b, whole_a))
    (grad_b,) = student_backward(y, forward, [sum_b, theirs_b], 1, start=part_kv)
    kept_b, sent_b = weight_grad(core, grad_b, rows)
    got_b = send_direct(list(pair_sum(row_blocks(), kept_b, shift(sent_b, "core"))))
    theirs = shift(lax.dynamic_index_in_dim(ring_a, 1 - ylo, 0, keepdims=False), "ylo")
    mine = lax.dynamic_index_in_dim(ring_a, ylo, 0, keepdims=False)
    return tuple(finish([mine, theirs], got_b))


def solution(mesh):
    fine = Mesh(mesh.devices.reshape(2, 4, 2, 4, 2), DP + TENSOR)
    placed = (
        P(DP, None, TENSOR),
        P(DP, None, TENSOR),
        P(DP, None, TENSOR),
        P(TENSOR, None),
        P(DP, TENSOR, None),
        P(DP, TENSOR),
        P(DP, TENSOR),
        P(DP, TENSOR),
    )
    return jax.shard_map(
        per_device,
        mesh=fine,
        in_specs=placed,
        out_specs=(P(DP, TENSOR), P(DP, TENSOR), P(DP, TENSOR)),
        check_vma=False,
    )
```

```python
import functools

import jax
import jax.numpy as jnp
from jax import lax
from jax.experimental import pallas as pl
from jax.experimental.pallas import tpu as pltpu
from jax.sharding import Mesh, PartitionSpec as P

HEAD = 128
FACTOR = HEAD ** (-0.5)
LOG2E = 1.4426950408889634
BLOCK = 256
SEQ = 1024
DP = ("ylo", "z", "core")
TENSOR = ("x", "yhi")
NT = (((1,), (1,)), ((), ()))
VMEM = pltpu.CompilerParams(vmem_limit_bytes=60 * 1024 * 1024)


def cost(us, moved=0):
    return pl.CostEstimate(flops=int(us * 1.0e9), bytes_accessed=moved, transcendentals=0)


def dot(a, b):
    return jnp.dot(a, b, preferred_element_type=jnp.float32)


def parts_of(number):
    first = number * BLOCK
    own = (first, first + BLOCK)
    return [(0, first), own] if first else [own]


def teacher_kernel(q_ref, k_ref, v_ref, o_ref):
    row = lax.broadcasted_iota(jnp.int32, (BLOCK, BLOCK), 0)
    col = lax.broadcasted_iota(jnp.int32, (BLOCK, BLOCK), 1)
    for number in range(SEQ // BLOCK):
        first = number * BLOCK
        limit = first + BLOCK
        parts = parts_of(number)
        for head in range(2):
            cols = slice(head * HEAD, head * HEAD + HEAD)
            queries = q_ref[first:limit, cols]
            scores = [
                lax.dot_general(queries, k_ref[lo:hi, :], NT, preferred_element_type=jnp.float32)
                for lo, hi in parts
            ]
            scores[-1] = jnp.where(col <= row, scores[-1], -1e30)
            top = functools.reduce(
                jnp.maximum, [jnp.max(s, axis=1, keepdims=True) for s in scores]
            )
            weights = [jnp.exp2((s - top) * (FACTOR * LOG2E)) for s in scores]
            total = sum(jnp.sum(w, axis=1, keepdims=True) for w in weights)
            context = sum(
                dot(w.astype(jnp.bfloat16), v_ref[lo:hi, :]) for w, (lo, hi) in zip(weights, parts)
            )
            o_ref[first:limit, cols] = (context / total).astype(jnp.bfloat16)


def teacher_attention(queries, keys, values, half, before=()):
    steps = queries.shape[1] // (4 * HEAD)
    pair = pl.BlockSpec((SEQ, 2 * HEAD), lambda h: (0, half * steps + h))
    one = pl.BlockSpec((SEQ, HEAD), lambda h: (0, 0))
    return pl.pallas_call(
        lambda q_ref, k_ref, v_ref, *rest: teacher_kernel(q_ref, k_ref, v_ref, rest[-1]),
        grid=(steps,),
        in_specs=[pair, one, one] + [pl.BlockSpec(memory_space=pl.ANY)] * len(before),
        out_specs=pair,
        out_shape=jax.ShapeDtypeStruct(queries.shape, jnp.bfloat16),
        input_output_aliases={3: 0} if before else {},
        compiler_params=VMEM,
        cost_estimate=cost(150 if before else 40),
        name="teacher_attention",
    )(queries, keys, values, *before)


def project_kernel(order_ref, context_ref, a_ref, b_ref, o_ref):
    o_ref[0] = dot(context_ref[...], a_ref[...]).astype(jnp.bfloat16)
    o_ref[1] = dot(context_ref[...], b_ref[...]).astype(jnp.bfloat16)


def project(order, context, projector, weight):
    rows = projector.shape[0]
    count = order.shape[0]
    return pl.pallas_call(
        project_kernel,
        grid_spec=pltpu.PrefetchScalarGridSpec(
            num_scalar_prefetch=1,
            grid=(count // 2,),
            in_specs=[
                pl.BlockSpec(context.shape, lambda g, order: (0, 0)),
                pl.BlockSpec((rows, 256), lambda g, order: (0, order[2 * g])),
                pl.BlockSpec((rows, 256), lambda g, order: (0, order[2 * g + 1])),
            ],
            out_specs=pl.BlockSpec((2, SEQ, 256), lambda g, order: (g, 0, 0)),
        ),
        out_shape=jax.ShapeDtypeStruct((count, SEQ, 256), jnp.bfloat16),
        compiler_params=VMEM,
        cost_estimate=cost(weight),
        name="project",
    )(order, context, projector, projector)


def student_project_kernel(count, *refs):
    at_ref, pieces, near_ref, far_ref = refs[0], refs[2 : 2 + count], refs[2 + count], refs[3 + count]
    o_ref, rows_ref, total = refs[-3:]
    step = pl.program_id(0)
    for number, ref in enumerate(pieces):
        rows_ref[pl.ds(pl.multiple_of(at_ref[number], 64), ref.shape[0]), :] = ref[...]

    @pl.when(step == 0)
    def _():
        total[...] = dot(rows_ref[...], near_ref[...])

    @pl.when(step == 1)
    def _():
        o_ref[...] = (total[...] + dot(rows_ref[...], far_ref[...])).astype(jnp.bfloat16)


def student_project(places, order, pieces, near, far, before=()):
    depth, cols = near.shape
    half = SEQ // 2
    block = depth
    side = 1 if before else 0
    count = len(pieces)
    return pl.pallas_call(
        lambda *refs: student_project_kernel(count, *refs),
        grid_spec=pltpu.PrefetchScalarGridSpec(
            num_scalar_prefetch=2,
            grid=(2,),
            in_specs=[
                pl.BlockSpec((p.shape[0], block), lambda k, at, order: (0, order[k]))
                for p in pieces
            ]
            + [
                pl.BlockSpec((block, cols), lambda k, at, order: (0, 0)),
                pl.BlockSpec((block, cols), lambda k, at, order: (0, 0)),
            ]
            + [pl.BlockSpec(memory_space=pl.ANY)] * len(before),
            out_specs=[
                pl.BlockSpec((half, cols), lambda k, at, order: (side, 0)),
                pl.BlockSpec((half, block), lambda k, at, order: (side, order[k])),
            ],
            scratch_shapes=[pltpu.VMEM((half, cols), jnp.float32)],
        ),
        out_shape=[
            jax.ShapeDtypeStruct((SEQ, cols), jnp.bfloat16),
            jax.ShapeDtypeStruct((SEQ, 2 * depth), jnp.bfloat16),
        ],
        input_output_aliases={4 + count: 0, 5 + count: 1} if before else {},
        compiler_params=VMEM,
        cost_estimate=cost(9 if before else 0),
        name="student_project",
    )(places, order, *pieces, near, far, *before)


def weight_grad_ring_kernel(grad_ref, rows_ref, o_ref):
    product = dot(grad_ref[...], rows_ref[...]).astype(jnp.bfloat16)
    for z in range(2):
        for core in range(2):
            at = (2 * z + core) * 256
            o_ref[z, core, 0] = product[:, at : at + 256]


def weight_grad_ring(grads, rows):
    cols = grads.shape[0]
    return pl.pallas_call(
        weight_grad_ring_kernel,
        grid=(4,),
        in_specs=[
            pl.BlockSpec(grads.shape, lambda k: (0, 0)),
            pl.BlockSpec((SEQ, 1024), lambda k: (0, k)),
        ],
        out_specs=pl.BlockSpec((2, 2, 1, cols, 256), lambda k: (k % 2, 0, k // 2, 0, 0)),
        out_shape=jax.ShapeDtypeStruct((4, 2, 2, cols, 256), jnp.bfloat16),
        compiler_params=VMEM,
        cost_estimate=cost(4),
        name="weight_grad_ring",
    )(grads, rows)


def weight_grad_kernel(core_ref, grad_ref, rows_ref, kept_ref, sent_ref):
    product = dot(grad_ref[...], rows_ref[...]).astype(jnp.bfloat16)

    def store(first, second):
        for z in range(2):
            first[z] = product[:, 512 * z : 512 * z + 256]
            second[z] = product[:, 512 * z + 256 : 512 * z + 512]

    @pl.when(core_ref[0] == 0)
    def _():
        store(kept_ref, sent_ref)

    @pl.when(core_ref[0] == 1)
    def _():
        store(sent_ref, kept_ref)


def weight_grad(core, grads, rows):
    cols = grads.shape[0]
    out = pl.BlockSpec((2, cols, 256), lambda k, core: (k, 0, 0))
    return pl.pallas_call(
        weight_grad_kernel,
        grid_spec=pltpu.PrefetchScalarGridSpec(
            num_scalar_prefetch=1,
            grid=(4,),
            in_specs=[
                pl.BlockSpec(grads.shape, lambda k, core: (0, 0)),
                pl.BlockSpec((SEQ, 1024), lambda k, core: (0, k)),
            ],
            out_specs=[out, out],
        ),
        out_shape=[jax.ShapeDtypeStruct((8, cols, 256), jnp.bfloat16)] * 2,
        compiler_params=VMEM,
        cost_estimate=cost(4),
        name="weight_grad",
    )(core, grads, rows)


def pair_kernel(order_ref, a_ref, b_ref, *outs):
    for number, ref in enumerate(outs):
        at = order_ref[number]
        ref[...] = (a_ref[at].astype(jnp.float32) + b_ref[at].astype(jnp.float32)).astype(
            jnp.bfloat16
        )


def pair_sum(order, a, b):
    whole = pl.BlockSpec(a.shape, lambda i, order: (0, 0, 0))
    one = pl.BlockSpec(a.shape[1:], lambda i, order: (0, 0))
    return pl.pallas_call(
        pair_kernel,
        grid_spec=pltpu.PrefetchScalarGridSpec(
            num_scalar_prefetch=1,
            grid=(1,),
            in_specs=[whole, whole],
            out_specs=[one] * a.shape[0],
        ),
        out_shape=[jax.ShapeDtypeStruct(a.shape[1:], jnp.bfloat16) for _ in range(a.shape[0])],
        compiler_params=VMEM,
        cost_estimate=cost(3),
        name="pair_sum",
    )(order, a, b)


def forward_kernel(y_ref, q_in, k_in, v_in, q_ref, kv_ref, probs_ref, context_ref, vt):
    y = y_ref[0]
    for block in range(4):
        for which, side in ((0, y), (1, 1 - y)):
            rows = slice((4 * which + block) * HEAD, (4 * which + block) * HEAD + HEAD)
            at = pl.ds(pl.multiple_of((2 * block + side) * HEAD, HEAD), HEAD)
            q_ref[at, :] = q_in[rows, :]
            kv_ref[at, :HEAD] = k_in[rows, :]
            kv_ref[at, HEAD:] = v_in[rows, :]
    vt[...] = kv_ref[:, HEAD:].T
    key = lax.broadcasted_iota(jnp.int32, (BLOCK, BLOCK), 0)
    query = lax.broadcasted_iota(jnp.int32, (BLOCK, BLOCK), 1)
    for number in range(SEQ // BLOCK):
        first = number * BLOCK
        limit = first + BLOCK
        parts = parts_of(number)
        for head in range(2):
            cols = slice(head * HEAD, head * HEAD + HEAD)
            queries = q_ref[first:limit, cols]
            scores = [
                lax.dot_general(
                    kv_ref[lo:hi, :HEAD], queries, NT, preferred_element_type=jnp.float32
                )
                for lo, hi in parts
            ]
            scores[-1] = jnp.where(key <= query, scores[-1], -1e30)
            top = functools.reduce(
                jnp.maximum, [jnp.max(s, axis=0, keepdims=True) for s in scores]
            )
            weights = [jnp.exp2((s - top) * (FACTOR * LOG2E)) for s in scores]
            scale = 1.0 / sum(jnp.sum(w, axis=0, keepdims=True) for w in weights)
            context = 0.0
            for w, (lo, hi) in zip(weights, parts):
                rounded = (w * scale).astype(jnp.bfloat16)
                probs_ref[head, lo:hi, first:limit] = rounded
                context += dot(vt[:, lo:hi], rounded)
            context_ref[first:limit, cols] = context.T


def student_forward(y, projected):
    pair = pl.BlockSpec((SEQ, 2 * HEAD), lambda i, y: (0, i))
    both = pl.BlockSpec((SEQ, 2 * HEAD), lambda i, y: (0, 0))
    return pl.pallas_call(
        forward_kernel,
        grid_spec=pltpu.PrefetchScalarGridSpec(
            num_scalar_prefetch=1,
            grid=(2,),
            in_specs=[
                pair,
                pl.BlockSpec((SEQ, HEAD), lambda i, y: (0, 4)),
                pl.BlockSpec((SEQ, HEAD), lambda i, y: (0, 5)),
            ],
            out_specs=[pair, both, pl.BlockSpec((2, SEQ, SEQ), lambda i, y: (i, 0, 0)), pair],
            scratch_shapes=[pltpu.VMEM((HEAD, SEQ), jnp.bfloat16)],
        ),
        out_shape=[
            jax.ShapeDtypeStruct((SEQ, 4 * HEAD), jnp.bfloat16),
            jax.ShapeDtypeStruct((SEQ, 2 * HEAD), jnp.bfloat16),
            jax.ShapeDtypeStruct((4, SEQ, SEQ), jnp.bfloat16),
            jax.ShapeDtypeStruct((SEQ, 4 * HEAD), jnp.float32),
        ],
        compiler_params=VMEM,
        cost_estimate=cost(60),
        name="student_forward",
    )(y, projected, projected, projected)


def backward_kernel(count, has_start, y_ref, q_ref, kv_ref, probs_ref, context_ref, *rest):
    targets, rest = rest[:count], rest[count:]
    if has_start:
        start_ref, grad_ref, kt, dk, dv = rest
        dk[...] = start_ref[:, :HEAD]
        dv[...] = start_ref[:, HEAD:]
    else:
        grad_ref, gkv_ref, kt, dk, dv = rest
        dk[...] = jnp.zeros_like(dk)
        dv[...] = jnp.zeros_like(dv)
    y = y_ref[0]
    kt[...] = kv_ref[:, :HEAD].T

    def store(at, block, value):
        for which, side in ((0, y), (1, 1 - y)):
            lanes = pl.ds(pl.multiple_of((4 * side + block) * HEAD, HEAD), HEAD)
            grad_ref[at, lanes] = value[:, which * HEAD : which * HEAD + HEAD]

    for number in range(SEQ // BLOCK):
        first = number * BLOCK
        limit = first + BLOCK
        parts = parts_of(number)
        for head in range(2):
            cols = slice(head * HEAD, head * HEAD + HEAD)
            queries = q_ref[first:limit, cols]
            target = 0.0
            for part in targets:
                target += part[0, first:limit, cols].astype(jnp.float32)
            incoming = ((context_ref[first:limit, cols] - target) * (1.0 / 16)).astype(
                jnp.bfloat16
            )
            rounded = [probs_ref[head, lo:hi, first:limit] for lo, hi in parts]
            probs = [r.astype(jnp.float32) for r in rounded]
            grad_probs = [
                lax.dot_general(
                    kv_ref[lo:hi, HEAD:], incoming, NT, preferred_element_type=jnp.float32
                )
                for lo, hi in parts
            ]
            inner = sum(
                jnp.sum(g * p, axis=0, keepdims=True) for g, p in zip(grad_probs, probs)
            )
            scaled = [
                (p * (g - inner)).astype(jnp.bfloat16) for g, p in zip(grad_probs, probs)
            ]
            for r, s, (lo, hi) in zip(rounded, scaled, parts):
                dv[lo:hi, :] += dot(r, incoming)
                dk[lo:hi, :] += dot(s, queries)
            grad = sum(dot(kt[:, lo:hi], s) for s, (lo, hi) in zip(scaled, parts))
            store(cols, number, (grad * FACTOR).astype(jnp.bfloat16))

    if has_start:
        for number in range(SEQ // BLOCK):
            rows = slice(number * BLOCK, number * BLOCK + BLOCK)
            store(slice(256, 384), number, (dk[rows, :] * FACTOR).T.astype(jnp.bfloat16))
            store(slice(384, 512), number, dv[rows, :].T.astype(jnp.bfloat16))
    else:
        gkv_ref[:, :HEAD] = dk[...]
        gkv_ref[:, HEAD:] = dv[...]


def student_backward(y, forward, targets, part, start=None):
    queries, kv, probs, context = forward
    pair = pl.BlockSpec((SEQ, 2 * HEAD), lambda i, y: (0, part))
    whole = pl.BlockSpec((SEQ, 2 * HEAD), lambda i, y: (0, 0))
    columns = 256 if start is None else 512
    grad = pl.BlockSpec((columns, SEQ), lambda i, y: (0, 0))
    grad_shape = jax.ShapeDtypeStruct((columns, SEQ), jnp.bfloat16)
    at_side = pl.BlockSpec((1, SEQ, 2 * HEAD), lambda i, y: (y[0], 0, 0))
    alone = pl.BlockSpec((1, SEQ, 2 * HEAD), lambda i, y: (0, 0, 0))
    return pl.pallas_call(
        lambda *refs: backward_kernel(len(targets), start is not None, *refs),
        grid_spec=pltpu.PrefetchScalarGridSpec(
            num_scalar_prefetch=1,
            grid=(1,),
            in_specs=[pair, whole, pl.BlockSpec((2, SEQ, SEQ), lambda i, y: (part, 0, 0)), pair]
            + [alone if t.shape[0] == 1 else at_side for t in targets]
            + [whole] * (start is not None),
            out_specs=[grad, whole] if start is None else [grad],
            scratch_shapes=[
                pltpu.VMEM((HEAD, SEQ), jnp.bfloat16),
                pltpu.VMEM((SEQ, HEAD), jnp.float32),
                pltpu.VMEM((SEQ, HEAD), jnp.float32),
            ],
        ),
        out_shape=[grad_shape, jax.ShapeDtypeStruct((SEQ, 2 * HEAD), jnp.float32)]
        if start is None
        else [grad_shape],
        compiler_params=VMEM,
        cost_estimate=cost(8),
        name="student_backward",
    )(y, queries, kv, probs, context, *targets, *([] if start is None else [start]))


def shift(array, axis, step=1):
    n = lax.axis_size(axis)
    return lax.ppermute(array, axis, [(i, (i + step) % n) for i in range(n)])


def gather_rows_near(own):
    return shift(own, "yhi"), shift(own, "x", 1), shift(own, "x", -1)


def far_halves(left, right):
    half = left.shape[0] // 2
    return shift(left[:half], "x", 1), shift(right[half:], "x", -1)


def row_places(x):
    places = [(x + dx) % 4 * 128 + offset for dx, offset in ((0, 0), (3, 0), (1, 0), (2, 0), (2, 64))]
    return jnp.stack(places).astype(jnp.int32)


RELATIVE = [(0, 0), (0, 1), (0, 3), (1, 2), (1, 1), (1, 3), (1, 0), (0, 2)]


def row_blocks():
    y = lax.axis_index("ylo")
    z = lax.axis_index("z")
    return jnp.stack([(y + dy) % 2 * 4 + (z + dz) % 4 for dy, dz in RELATIVE]).astype(jnp.int32)


def send_direct(blocks):
    got = [blocks[0]]
    for (dy, dz), block in zip(RELATIVE[1:], blocks[1:]):
        route = [(i * 4 + k, (i + dy) % 2 * 4 + (k + dz) % 4) for i in range(2) for k in range(4)]
        got.append(lax.ppermute(block, ("ylo", "z"), route))
    return got


def finish_kernel(*refs):
    a_refs, b_refs, (q_ref, k_ref, v_ref) = refs[:2], refs[2:10], refs[10:]

    def total(parts):
        result = parts[0][...].astype(jnp.float32)
        for part in parts[1:]:
            result += part[...].astype(jnp.float32)
        return result.T

    q_ref[:, :256] = total(a_refs)
    rest = total(b_refs)
    q_ref[:, 256:] = rest[:, :256]
    k_ref[...] = rest[:, 256:384]
    v_ref[...] = rest[:, 384:]


def finish(got_a, got_b):
    return pl.pallas_call(
        finish_kernel,
        out_shape=[jax.ShapeDtypeStruct((256, cols), jnp.float32) for cols in (512, 128, 128)],
        compiler_params=VMEM,
        cost_estimate=cost(3),
        name="finish",
    )(*got_a, *got_b)


def per_device(
    teacher_queries,
    teacher_keys,
    teacher_values,
    projector,
    student_inputs,
    query_weight,
    key_weight,
    value_weight,
):
    tq, tk, tv = teacher_queries[0], teacher_keys[0], teacher_values[0]
    x, yhi, ylo = lax.axis_index("x"), lax.axis_index("yhi"), lax.axis_index("ylo")
    own = student_inputs[0]
    other, left, right = gather_rows_near(own)

    groups = jnp.arange(4, dtype=jnp.int32)
    context = teacher_attention(tq, tk, tv, 0)
    context, query_weight, key_weight, value_weight = lax.optimization_barrier(
        (context, query_weight, key_weight, value_weight)
    )
    shard = jnp.concatenate([query_weight, key_weight, value_weight], axis=1)
    near = lax.all_gather(shard, ("z", "core"), axis=0, tiled=True)
    shard_far = shift(shard, "ylo")
    context = teacher_attention(tq, tk, tv, 1, (context,))
    sent = project(2 * (2 * groups + 1 - yhi), context, projector, 0)
    context, left, right, other, sent, shard_far = lax.optimization_barrier(
        (context, left, right, other, sent, shard_far)
    )
    far = lax.all_gather(shard_far, ("z", "core"), axis=0, tiled=True)
    came = shift(sent, "yhi")
    own_far = far_halves(left, right)
    other_left, other_right = shift(other, "x", 1), shift(other, "x", -1)

    product_b = project(2 * jnp.arange(8, dtype=jnp.int32) + 1, context, projector, 0)
    sum_b = lax.psum_scatter(product_b, "x", scatter_dimension=0, tiled=True)
    context, other_left, other_right, own_far, product_b = lax.optimization_barrier(
        (context, other_left, other_right, own_far, product_b)
    )
    kept = project(2 * (2 * groups + yhi), context, projector, 30)
    other_far = far_halves(other_left, other_right)

    places = row_places(x)
    order = jnp.stack([ylo, 1 - ylo]).astype(jnp.int32)
    before = student_project(places, order, [own, left, right, *own_far], near, far)
    came, before = lax.optimization_barrier((came, before))
    by_x = ((x + jnp.arange(4)) % 4).astype(jnp.int32)
    blocks_a = pair_sum(by_x, kept, came)
    targets_a = [blocks_a[0][None]] + [
        shift(block, "x", step)[None] for step, block in enumerate(blocks_a) if step
    ]
    projected, rows = student_project(
        places, order, [other, other_left, other_right, *other_far], near, far, before
    )

    y = yhi.astype(jnp.int32).reshape(1)
    core = lax.axis_index("core").astype(jnp.int32).reshape(1)
    forward = student_forward(y, projected)
    forward, targets_a = lax.optimization_barrier((forward, targets_a))

    grad_a, part_kv = student_backward(y, forward, targets_a, 0)
    sum_b, grad_a = lax.optimization_barrier((sum_b, grad_a))
    theirs_b = shift(lax.dynamic_slice_in_dim(sum_b, 1 - yhi, 1, 0), "yhi")
    whole_a = weight_grad_ring(grad_a, rows)
    ring_a = lax.psum_scatter(
        whole_a.reshape(16, 256, 256), ("z", "core"), scatter_dimension=0, tiled=True
    )
    theirs_b, whole_a = lax.optimization_barrier((theirs_b, whole_a))
    (grad_b,) = student_backward(y, forward, [sum_b, theirs_b], 1, start=part_kv)
    kept_b, sent_b = weight_grad(core, grad_b, rows)
    got_b = send_direct(list(pair_sum(row_blocks(), kept_b, shift(sent_b, "core"))))
    theirs = shift(lax.dynamic_index_in_dim(ring_a, 1 - ylo, 0, keepdims=False), "ylo")
    mine = lax.dynamic_index_in_dim(ring_a, ylo, 0, keepdims=False)
    return tuple(finish([mine, theirs], got_b))


def solution(mesh):
    fine = Mesh(mesh.devices.reshape(2, 4, 2, 4, 2), DP + TENSOR)
    placed = (
        P(DP, None, TENSOR),
        P(DP, None, TENSOR),
        P(DP, None, TENSOR),
        P(TENSOR, None),
        P(DP, TENSOR, None),
        P(DP, TENSOR),
        P(DP, TENSOR),
        P(DP, TENSOR),
    )
    return jax.shard_map(
        per_device,
        mesh=fine,
        in_specs=placed,
        out_specs=(P(DP, TENSOR), P(DP, TENSOR), P(DP, TENSOR)),
        check_vma=False,
    )
```

```python
import functools

import jax
import jax.numpy as jnp
from jax import lax
from jax.experimental import pallas as pl
from jax.experimental.pallas import tpu as pltpu
from jax.sharding import Mesh, PartitionSpec as P

HEAD = 128
FACTOR = HEAD ** (-0.5)
LOG2E = 1.4426950408889634
BLOCK = 256
SEQ = 1024
DP = ("ylo", "z", "core")
TENSOR = ("x", "yhi")
NT = (((1,), (1,)), ((), ()))
VMEM = pltpu.CompilerParams(vmem_limit_bytes=60 * 1024 * 1024)


def cost(us, moved=0):
    return pl.CostEstimate(flops=int(us * 1.0e9), bytes_accessed=moved, transcendentals=0)


def dot(a, b):
    return jnp.dot(a, b, preferred_element_type=jnp.float32)


def parts_of(number):
    first = number * BLOCK
    own = (first, first + BLOCK)
    return [(0, first), own] if first else [own]


def teacher_kernel(q_ref, k_ref, v_ref, o_ref):
    row = lax.broadcasted_iota(jnp.int32, (BLOCK, BLOCK), 0)
    col = lax.broadcasted_iota(jnp.int32, (BLOCK, BLOCK), 1)
    for number in range(SEQ // BLOCK):
        first = number * BLOCK
        limit = first + BLOCK
        parts = parts_of(number)
        queries = q_ref[first:limit, :]
        scores = [
            lax.dot_general(queries, k_ref[lo:hi, :], NT, preferred_element_type=jnp.float32)
            for lo, hi in parts
        ]
        scores[-1] = jnp.where(col <= row, scores[-1], -1e30)
        top = functools.reduce(
            jnp.maximum, [jnp.max(s, axis=1, keepdims=True) for s in scores]
        )
        weights = [jnp.exp2((s - top) * (FACTOR * LOG2E)) for s in scores]
        total = sum(jnp.sum(w, axis=1, keepdims=True) for w in weights)
        context = sum(
            dot(w.astype(jnp.bfloat16), v_ref[lo:hi, :]) for w, (lo, hi) in zip(weights, parts)
        )
        o_ref[first:limit, :] = (context / total).astype(jnp.bfloat16)


def teacher_attention(queries, keys, values, half, before=()):
    steps = queries.shape[1] // (2 * HEAD)
    each = pl.BlockSpec((SEQ, HEAD), lambda h: (0, half * steps + h))
    one = pl.BlockSpec((SEQ, HEAD), lambda h: (0, 0))
    return pl.pallas_call(
        lambda q_ref, k_ref, v_ref, *rest: teacher_kernel(q_ref, k_ref, v_ref, rest[-1]),
        grid=(steps,),
        in_specs=[each, one, one] + [pl.BlockSpec(memory_space=pl.ANY)] * len(before),
        out_specs=each,
        out_shape=jax.ShapeDtypeStruct(queries.shape, jnp.bfloat16),
        input_output_aliases={3: 0} if before else {},
        compiler_params=VMEM,
        cost_estimate=cost(150 if before else 40),
        name="teacher_attention",
    )(queries, keys, values, *before)


def project_kernel(order_ref, context_ref, a_ref, b_ref, o_ref):
    o_ref[0] = dot(context_ref[...], a_ref[...]).astype(jnp.bfloat16)
    o_ref[1] = dot(context_ref[...], b_ref[...]).astype(jnp.bfloat16)


def project(order, context, projector, weight):
    rows = projector.shape[0]
    count = order.shape[0]
    return pl.pallas_call(
        project_kernel,
        grid_spec=pltpu.PrefetchScalarGridSpec(
            num_scalar_prefetch=1,
            grid=(count // 2,),
            in_specs=[
                pl.BlockSpec(context.shape, lambda g, order: (0, 0)),
                pl.BlockSpec((rows, 256), lambda g, order: (0, order[2 * g])),
                pl.BlockSpec((rows, 256), lambda g, order: (0, order[2 * g + 1])),
            ],
            out_specs=pl.BlockSpec((2, SEQ, 256), lambda g, order: (g, 0, 0)),
        ),
        out_shape=jax.ShapeDtypeStruct((count, SEQ, 256), jnp.bfloat16),
        compiler_params=VMEM,
        cost_estimate=cost(weight),
        name="project",
    )(order, context, projector, projector)


def student_project_kernel(count, *refs):
    at_ref, pieces, near_ref, far_ref = refs[0], refs[2 : 2 + count], refs[2 + count], refs[3 + count]
    o_ref, rows_ref, total = refs[-3:]
    step = pl.program_id(0)
    for number, ref in enumerate(pieces):
        rows_ref[pl.ds(pl.multiple_of(at_ref[number], 64), ref.shape[0]), :] = ref[...]

    @pl.when(step == 0)
    def _():
        total[...] = dot(rows_ref[...], near_ref[...])

    @pl.when(step == 1)
    def _():
        o_ref[...] = (total[...] + dot(rows_ref[...], far_ref[...])).astype(jnp.bfloat16)


def student_project(places, order, pieces, near, far, before=()):
    depth, cols = near.shape
    half = SEQ // 2
    block = depth
    side = 1 if before else 0
    count = len(pieces)
    return pl.pallas_call(
        lambda *refs: student_project_kernel(count, *refs),
        grid_spec=pltpu.PrefetchScalarGridSpec(
            num_scalar_prefetch=2,
            grid=(2,),
            in_specs=[
                pl.BlockSpec((p.shape[0], block), lambda k, at, order: (0, order[k]))
                for p in pieces
            ]
            + [
                pl.BlockSpec((block, cols), lambda k, at, order: (0, 0)),
                pl.BlockSpec((block, cols), lambda k, at, order: (0, 0)),
            ]
            + [pl.BlockSpec(memory_space=pl.ANY)] * len(before),
            out_specs=[
                pl.BlockSpec((half, cols), lambda k, at, order: (side, 0)),
                pl.BlockSpec((half, block), lambda k, at, order: (side, order[k])),
            ],
            scratch_shapes=[pltpu.VMEM((half, cols), jnp.float32)],
        ),
        out_shape=[
            jax.ShapeDtypeStruct((SEQ, cols), jnp.bfloat16),
            jax.ShapeDtypeStruct((SEQ, 2 * depth), jnp.bfloat16),
        ],
        input_output_aliases={4 + count: 0, 5 + count: 1} if before else {},
        compiler_params=VMEM,
        cost_estimate=cost(9 if before else 0),
        name="student_project",
    )(places, order, *pieces, near, far, *before)


def weight_grad_ring_kernel(grad_ref, rows_ref, o_ref):
    product = dot(grad_ref[...], rows_ref[...]).astype(jnp.bfloat16)
    for z in range(2):
        for core in range(2):
            at = (2 * z + core) * 256
            o_ref[z, core, 0] = product[:, at : at + 256]


def weight_grad_ring(grads, rows):
    cols = grads.shape[0]
    return pl.pallas_call(
        weight_grad_ring_kernel,
        grid=(4,),
        in_specs=[
            pl.BlockSpec(grads.shape, lambda k: (0, 0)),
            pl.BlockSpec((SEQ, 1024), lambda k: (0, k)),
        ],
        out_specs=pl.BlockSpec((2, 2, 1, cols, 256), lambda k: (k % 2, 0, k // 2, 0, 0)),
        out_shape=jax.ShapeDtypeStruct((4, 2, 2, cols, 256), jnp.bfloat16),
        compiler_params=VMEM,
        cost_estimate=cost(4),
        name="weight_grad_ring",
    )(grads, rows)


def weight_grad_kernel(core_ref, grad_ref, rows_ref, kept_ref, sent_ref):
    product = dot(grad_ref[...], rows_ref[...]).astype(jnp.bfloat16)

    def store(first, second):
        for z in range(2):
            first[z] = product[:, 512 * z : 512 * z + 256]
            second[z] = product[:, 512 * z + 256 : 512 * z + 512]

    @pl.when(core_ref[0] == 0)
    def _():
        store(kept_ref, sent_ref)

    @pl.when(core_ref[0] == 1)
    def _():
        store(sent_ref, kept_ref)


def weight_grad(core, grads, rows):
    cols = grads.shape[0]
    out = pl.BlockSpec((2, cols, 256), lambda k, core: (k, 0, 0))
    return pl.pallas_call(
        weight_grad_kernel,
        grid_spec=pltpu.PrefetchScalarGridSpec(
            num_scalar_prefetch=1,
            grid=(4,),
            in_specs=[
                pl.BlockSpec(grads.shape, lambda k, core: (0, 0)),
                pl.BlockSpec((SEQ, 1024), lambda k, core: (0, k)),
            ],
            out_specs=[out, out],
        ),
        out_shape=[jax.ShapeDtypeStruct((8, cols, 256), jnp.bfloat16)] * 2,
        compiler_params=VMEM,
        cost_estimate=cost(4),
        name="weight_grad",
    )(core, grads, rows)


def pair_kernel(order_ref, a_ref, b_ref, *outs):
    for number, ref in enumerate(outs):
        at = order_ref[number]
        ref[...] = (a_ref[at].astype(jnp.float32) + b_ref[at].astype(jnp.float32)).astype(
            jnp.bfloat16
        )


def pair_sum(order, a, b):
    whole = pl.BlockSpec(a.shape, lambda i, order: (0, 0, 0))
    one = pl.BlockSpec(a.shape[1:], lambda i, order: (0, 0))
    return pl.pallas_call(
        pair_kernel,
        grid_spec=pltpu.PrefetchScalarGridSpec(
            num_scalar_prefetch=1,
            grid=(1,),
            in_specs=[whole, whole],
            out_specs=[one] * a.shape[0],
        ),
        out_shape=[jax.ShapeDtypeStruct(a.shape[1:], jnp.bfloat16) for _ in range(a.shape[0])],
        compiler_params=VMEM,
        cost_estimate=cost(3),
        name="pair_sum",
    )(order, a, b)


def forward_kernel(y_ref, q_in, k_in, v_in, q_ref, kv_ref, probs_ref, context_ref, vt):
    y = y_ref[0]
    for block in range(4):
        for which, side in ((0, y), (1, 1 - y)):
            rows = slice((4 * which + block) * HEAD, (4 * which + block) * HEAD + HEAD)
            at = pl.ds(pl.multiple_of((2 * block + side) * HEAD, HEAD), HEAD)
            q_ref[at, :] = q_in[rows, :]
            kv_ref[at, :HEAD] = k_in[rows, :]
            kv_ref[at, HEAD:] = v_in[rows, :]
    vt[...] = kv_ref[:, HEAD:].T
    key = lax.broadcasted_iota(jnp.int32, (BLOCK, BLOCK), 0)
    query = lax.broadcasted_iota(jnp.int32, (BLOCK, BLOCK), 1)
    for number in range(SEQ // BLOCK):
        first = number * BLOCK
        limit = first + BLOCK
        parts = parts_of(number)
        for head in range(2):
            cols = slice(head * HEAD, head * HEAD + HEAD)
            queries = q_ref[first:limit, cols]
            scores = [
                lax.dot_general(
                    kv_ref[lo:hi, :HEAD], queries, NT, preferred_element_type=jnp.float32
                )
                for lo, hi in parts
            ]
            scores[-1] = jnp.where(key <= query, scores[-1], -1e30)
            top = functools.reduce(
                jnp.maximum, [jnp.max(s, axis=0, keepdims=True) for s in scores]
            )
            weights = [jnp.exp2((s - top) * (FACTOR * LOG2E)) for s in scores]
            scale = 1.0 / sum(jnp.sum(w, axis=0, keepdims=True) for w in weights)
            context = 0.0
            for w, (lo, hi) in zip(weights, parts):
                rounded = (w * scale).astype(jnp.bfloat16)
                probs_ref[head, lo:hi, first:limit] = rounded
                context += dot(vt[:, lo:hi], rounded)
            context_ref[first:limit, cols] = context.T


def student_forward(y, projected):
    pair = pl.BlockSpec((SEQ, 2 * HEAD), lambda i, y: (0, i))
    both = pl.BlockSpec((SEQ, 2 * HEAD), lambda i, y: (0, 0))
    return pl.pallas_call(
        forward_kernel,
        grid_spec=pltpu.PrefetchScalarGridSpec(
            num_scalar_prefetch=1,
            grid=(2,),
            in_specs=[
                pair,
                pl.BlockSpec((SEQ, HEAD), lambda i, y: (0, 4)),
                pl.BlockSpec((SEQ, HEAD), lambda i, y: (0, 5)),
            ],
            out_specs=[pair, both, pl.BlockSpec((2, SEQ, SEQ), lambda i, y: (i, 0, 0)), pair],
            scratch_shapes=[pltpu.VMEM((HEAD, SEQ), jnp.bfloat16)],
        ),
        out_shape=[
            jax.ShapeDtypeStruct((SEQ, 4 * HEAD), jnp.bfloat16),
            jax.ShapeDtypeStruct((SEQ, 2 * HEAD), jnp.bfloat16),
            jax.ShapeDtypeStruct((4, SEQ, SEQ), jnp.bfloat16),
            jax.ShapeDtypeStruct((SEQ, 4 * HEAD), jnp.float32),
        ],
        compiler_params=VMEM,
        cost_estimate=cost(60),
        name="student_forward",
    )(y, projected, projected, projected)


def backward_kernel(count, has_start, y_ref, q_ref, kv_ref, probs_ref, context_ref, *rest):
    targets, rest = rest[:count], rest[count:]
    if has_start:
        start_ref, grad_ref, kt, dk, dv = rest
        dk[...] = start_ref[:, :HEAD]
        dv[...] = start_ref[:, HEAD:]
    else:
        grad_ref, gkv_ref, kt, dk, dv = rest
        dk[...] = jnp.zeros_like(dk)
        dv[...] = jnp.zeros_like(dv)
    y = y_ref[0]
    kt[...] = kv_ref[:, :HEAD].T

    def store(at, block, value):
        for which, side in ((0, y), (1, 1 - y)):
            lanes = pl.ds(pl.multiple_of((4 * side + block) * HEAD, HEAD), HEAD)
            grad_ref[at, lanes] = value[:, which * HEAD : which * HEAD + HEAD]

    for number in range(SEQ // BLOCK):
        first = number * BLOCK
        limit = first + BLOCK
        parts = parts_of(number)
        for head in range(2):
            cols = slice(head * HEAD, head * HEAD + HEAD)
            queries = q_ref[first:limit, cols]
            target = 0.0
            for part in targets:
                target += part[0, first:limit, cols].astype(jnp.float32)
            incoming = ((context_ref[first:limit, cols] - target) * (1.0 / 16)).astype(
                jnp.bfloat16
            )
            rounded = [probs_ref[head, lo:hi, first:limit] for lo, hi in parts]
            probs = [r.astype(jnp.float32) for r in rounded]
            grad_probs = [
                lax.dot_general(
                    kv_ref[lo:hi, HEAD:], incoming, NT, preferred_element_type=jnp.float32
                )
                for lo, hi in parts
            ]
            inner = sum(
                jnp.sum(g * p, axis=0, keepdims=True) for g, p in zip(grad_probs, probs)
            )
            scaled = [
                (p * (g - inner)).astype(jnp.bfloat16) for g, p in zip(grad_probs, probs)
            ]
            for r, s, (lo, hi) in zip(rounded, scaled, parts):
                dv[lo:hi, :] += dot(r, incoming)
                dk[lo:hi, :] += dot(s, queries)
            grad = sum(dot(kt[:, lo:hi], s) for s, (lo, hi) in zip(scaled, parts))
            store(cols, number, (grad * FACTOR).astype(jnp.bfloat16))

    if has_start:
        for number in range(SEQ // BLOCK):
            rows = slice(number * BLOCK, number * BLOCK + BLOCK)
            store(slice(256, 384), number, (dk[rows, :] * FACTOR).T.astype(jnp.bfloat16))
            store(slice(384, 512), number, dv[rows, :].T.astype(jnp.bfloat16))
    else:
        gkv_ref[:, :HEAD] = dk[...]
        gkv_ref[:, HEAD:] = dv[...]


def student_backward(y, forward, targets, part, start=None):
    queries, kv, probs, context = forward
    pair = pl.BlockSpec((SEQ, 2 * HEAD), lambda i, y: (0, part))
    whole = pl.BlockSpec((SEQ, 2 * HEAD), lambda i, y: (0, 0))
    columns = 256 if start is None else 512
    grad = pl.BlockSpec((columns, SEQ), lambda i, y: (0, 0))
    grad_shape = jax.ShapeDtypeStruct((columns, SEQ), jnp.bfloat16)
    at_side = pl.BlockSpec((1, SEQ, 2 * HEAD), lambda i, y: (y[0], 0, 0))
    alone = pl.BlockSpec((1, SEQ, 2 * HEAD), lambda i, y: (0, 0, 0))
    return pl.pallas_call(
        lambda *refs: backward_kernel(len(targets), start is not None, *refs),
        grid_spec=pltpu.PrefetchScalarGridSpec(
            num_scalar_prefetch=1,
            grid=(1,),
            in_specs=[pair, whole, pl.BlockSpec((2, SEQ, SEQ), lambda i, y: (part, 0, 0)), pair]
            + [alone if t.shape[0] == 1 else at_side for t in targets]
            + [whole] * (start is not None),
            out_specs=[grad, whole] if start is None else [grad],
            scratch_shapes=[
                pltpu.VMEM((HEAD, SEQ), jnp.bfloat16),
                pltpu.VMEM((SEQ, HEAD), jnp.float32),
                pltpu.VMEM((SEQ, HEAD), jnp.float32),
            ],
        ),
        out_shape=[grad_shape, jax.ShapeDtypeStruct((SEQ, 2 * HEAD), jnp.float32)]
        if start is None
        else [grad_shape],
        compiler_params=VMEM,
        cost_estimate=cost(8),
        name="student_backward",
    )(y, queries, kv, probs, context, *targets, *([] if start is None else [start]))


def shift(array, axis, step=1):
    n = lax.axis_size(axis)
    return lax.ppermute(array, axis, [(i, (i + step) % n) for i in range(n)])


def gather_rows_near(own):
    return shift(own, "yhi"), shift(own, "x", 1), shift(own, "x", -1)


def far_halves(left, right):
    half = left.shape[0] // 2
    return shift(left[:half], "x", 1), shift(right[half:], "x", -1)


def row_places(x):
    places = [(x + dx) % 4 * 128 + offset for dx, offset in ((0, 0), (3, 0), (1, 0), (2, 0), (2, 64))]
    return jnp.stack(places).astype(jnp.int32)


RELATIVE = [(0, 0), (0, 2), (1, 2), (1, 1), (1, 3), (1, 0), (0, 1), (0, 3)]


def row_blocks():
    y = lax.axis_index("ylo")
    z = lax.axis_index("z")
    return jnp.stack([(y + dy) % 2 * 4 + (z + dz) % 4 for dy, dz in RELATIVE]).astype(jnp.int32)


def send_direct(blocks):
    got = [blocks[0]]
    for (dy, dz), block in zip(RELATIVE[1:], blocks[1:]):
        route = [(i * 4 + k, (i + dy) % 2 * 4 + (k + dz) % 4) for i in range(2) for k in range(4)]
        got.append(lax.ppermute(block, ("ylo", "z"), route))
    return got


def finish_kernel(*refs):
    a_refs, b_refs, (q_ref, k_ref, v_ref) = refs[:2], refs[2:10], refs[10:]

    def total(parts):
        result = parts[0][...].astype(jnp.float32)
        for part in parts[1:]:
            result += part[...].astype(jnp.float32)
        return result.T

    q_ref[:, :256] = total(a_refs)
    rest = total(b_refs)
    q_ref[:, 256:] = rest[:, :256]
    k_ref[...] = rest[:, 256:384]
    v_ref[...] = rest[:, 384:]


def finish(got_a, got_b):
    return pl.pallas_call(
        finish_kernel,
        out_shape=[jax.ShapeDtypeStruct((256, cols), jnp.float32) for cols in (512, 128, 128)],
        compiler_params=VMEM,
        cost_estimate=cost(3),
        name="finish",
    )(*got_a, *got_b)


def per_device(
    teacher_queries,
    teacher_keys,
    teacher_values,
    projector,
    student_inputs,
    query_weight,
    key_weight,
    value_weight,
):
    tq, tk, tv = teacher_queries[0], teacher_keys[0], teacher_values[0]
    x, yhi, ylo = lax.axis_index("x"), lax.axis_index("yhi"), lax.axis_index("ylo")
    own = student_inputs[0]
    other, left, right = gather_rows_near(own)

    groups = jnp.arange(4, dtype=jnp.int32)
    context = teacher_attention(tq, tk, tv, 0)
    context, query_weight, key_weight, value_weight = lax.optimization_barrier(
        (context, query_weight, key_weight, value_weight)
    )
    shard = jnp.concatenate([query_weight, key_weight, value_weight], axis=1)
    near = lax.all_gather(shard, ("z", "core"), axis=0, tiled=True)
    shard_far = shift(shard, "ylo")
    context = teacher_attention(tq, tk, tv, 1, (context,))
    sent = project(2 * (2 * groups + 1 - yhi), context, projector, 0)
    context, left, right, other, sent, shard_far = lax.optimization_barrier(
        (context, left, right, other, sent, shard_far)
    )
    far = lax.all_gather(shard_far, ("z", "core"), axis=0, tiled=True)
    came = shift(sent, "yhi")
    own_far = far_halves(left, right)
    other_left, other_right = shift(other, "x", 1), shift(other, "x", -1)

    product_b = project(2 * jnp.arange(8, dtype=jnp.int32) + 1, context, projector, 0)
    sum_b = lax.psum_scatter(product_b, "x", scatter_dimension=0, tiled=True)
    context, other_left, other_right, own_far, product_b = lax.optimization_barrier(
        (context, other_left, other_right, own_far, product_b)
    )
    kept = project(2 * (2 * groups + yhi), context, projector, 30)
    other_far = far_halves(other_left, other_right)

    places = row_places(x)
    order = jnp.stack([ylo, 1 - ylo]).astype(jnp.int32)
    before = student_project(places, order, [own, left, right, *own_far], near, far)
    came, before = lax.optimization_barrier((came, before))
    by_x = ((x + jnp.arange(4)) % 4).astype(jnp.int32)
    blocks_a = pair_sum(by_x, kept, came)
    targets_a = [blocks_a[0][None]] + [
        shift(block, "x", step)[None] for step, block in enumerate(blocks_a) if step
    ]
    projected, rows = student_project(
        places, order, [other, other_left, other_right, *other_far], near, far, before
    )

    y = yhi.astype(jnp.int32).reshape(1)
    core = lax.axis_index("core").astype(jnp.int32).reshape(1)
    forward = student_forward(y, projected)
    forward, targets_a = lax.optimization_barrier((forward, targets_a))

    grad_a, part_kv = student_backward(y, forward, targets_a, 0)
    sum_b, grad_a = lax.optimization_barrier((sum_b, grad_a))
    theirs_b = shift(lax.dynamic_slice_in_dim(sum_b, 1 - yhi, 1, 0), "yhi")
    whole_a = weight_grad_ring(grad_a, rows)
    ring_a = lax.psum_scatter(
        whole_a.reshape(16, 256, 256), ("z", "core"), scatter_dimension=0, tiled=True
    )
    theirs_b, whole_a = lax.optimization_barrier((theirs_b, whole_a))
    (grad_b,) = student_backward(y, forward, [sum_b, theirs_b], 1, start=part_kv)
    kept_b, sent_b = weight_grad(core, grad_b, rows)
    got_b = send_direct(list(pair_sum(row_blocks(), kept_b, shift(sent_b, "core"))))
    theirs = shift(lax.dynamic_index_in_dim(ring_a, 1 - ylo, 0, keepdims=False), "ylo")
    mine = lax.dynamic_index_in_dim(ring_a, ylo, 0, keepdims=False)
    return tuple(finish([mine, theirs], got_b))


def solution(mesh):
    fine = Mesh(mesh.devices.reshape(2, 4, 2, 4, 2), DP + TENSOR)
    placed = (
        P(DP, None, TENSOR),
        P(DP, None, TENSOR),
        P(DP, None, TENSOR),
        P(TENSOR, None),
        P(DP, TENSOR, None),
        P(DP, TENSOR),
        P(DP, TENSOR),
        P(DP, TENSOR),
    )
    return jax.shard_map(
        per_device,
        mesh=fine,
        in_specs=placed,
        out_specs=(P(DP, TENSOR), P(DP, TENSOR), P(DP, TENSOR)),
        check_vma=False,
    )
```
